32 devices in a mesh: dp: 4 (over z), head: 4 (over y, x), blk: 2 (over core).
Axes of the slice: x: 2, y: 2, z: 4, core: 2. Of those that a mesh axis runs over, the one named last changes fastest.
Arguments:
- block_in: bfloat16 [4, 2048, 2048], P('dp', ('head', 'blk')), may hold values from -6 to 6
- cotangent: bfloat16 [4, 2048, 2048], P('dp', ('head', 'blk')), may hold values from -6 to 6
- seg_lengths: int32 [4, 4], P('dp'), may hold values from 0 to 2048, as said below
- ln1_gain: bfloat16 [2048], replicated, may hold values from 0.5 to 1.5
- ln1_bias: bfloat16 [2048], replicated, may hold values from -1.5 to 1.5
- qkv_weight: bfloat16 [2048, 6144], P('dp'), may hold values from -0.125 to 0.125
- qkv_bias: bfloat16 [6144], replicated, may hold values from -1.5 to 1.5
- out_weight: bfloat16 [2048, 2048], P('dp'), may hold values from -1 to 1
- out_bias: bfloat16 [2048], replicated, may hold values from -1.5 to 1.5
- ln2_gain: bfloat16 [2048], replicated, may hold values from 0.5 to 1.5
- ln2_bias: bfloat16 [2048], replicated, may hold values from -1.5 to 1.5
- fc1_weight: bfloat16 [2048, 8192], P('dp'), may hold values from -0.125 to 0.125
- fc1_bias: bfloat16 [8192], replicated, may hold values from -1.5 to 1.5
- fc2_weight: bfloat16 [2048, 8192], P('dp'), may hold values from -0.0625 to 0.0625
- fc2_bias: bfloat16 [2048], replicated, may hold values from -1.5 to 1.5
Outputs:
- block_out: bfloat16 [4, 2048, 2048], P('dp', ('head', 'blk'))
- input_grad: bfloat16 [4, 2048, 2048], P('dp', ('head', 'blk'))
- ln1_gain_grad: float32 [2048], replicated
- ln1_bias_grad: float32 [2048], replicated
- qkv_weight_grad: float32 [2048, 6144], P('dp')
- qkv_bias_grad: float32 [6144], replicated
- out_weight_grad: float32 [2048, 2048], P('dp')
- out_bias_grad: float32 [2048], replicated
- ln2_gain_grad: float32 [2048], replicated
- ln2_bias_grad: float32 [2048], replicated
- fc1_weight_grad: float32 [2048, 8192], P('dp')
- fc1_bias_grad: float32 [8192], replicated
- fc2_weight_grad: float32 [2048, 8192], P('dp')
- fc2_bias_grad: float32 [2048], replicated
- attn_rms: float32 [], replicated
- mlp_rms: float32 [], replicated
The draws below stay inside these ranges and needn't reach their ends.
Inputs may be any that keep to these rules, and one draw needn't show every extreme that they name: `seg_lengths`: each row lists one to four segment lengths, each 512, 1024 or 2048, that sum to 2048, followed by zeros; some row holds a single segment of 2048 tokens.
All inputs are finite; a program needn't handle non-finite values.
Results may differ from the reference program's by a relative error of at most 0.017.
Values may be sent and summed in bfloat16 or wider, within the bound.
No kernel may reach another device: no remote copies, remote signals or barrier semaphores. Data moves between devices by JAX's collectives and lax.ppermute only.
A program may use at most 768 MiB of HBM per device.

```python
import jax
import jax.numpy as jnp
from jax import lax

D = 2048
HEADS = 8
HEAD_SIZE = 256
ROT = 64
FF = 8192
ROW_LEN = 2048
ROWS = 4


def draw_seg_lengths(key, part):
    key = jax.random.fold_in(key, 11)
    pattern_key, whole_key = jax.random.split(key)
    patterns = jnp.array([[4, 0, 0, 0], [2, 2, 0, 0], [2, 1, 1, 0], [1, 2, 1, 0], [1, 1, 2, 0], [1, 1, 1, 1]], dtype=jnp.int32)
    picked = jax.random.randint(pattern_key, (ROWS,), 0, 6)
    whole_row = jax.random.randint(whole_key, (), 0, ROWS)
    picked = jnp.where(jnp.arange(ROWS) == whole_row, 0, picked)
    return (patterns[picked] * (ROW_LEN // 4)).astype(jnp.int32)


def raised(values, key, source, target, shards_of, factor):
    def block_of(axis_at):
        return (jnp.arange(values.shape[axis_at]) // (values.shape[axis_at] // shards_of)).reshape((-1,) + (1,) * (values.ndim - 1 - axis_at))

    first = jax.random.permutation(key, shards_of)[block_of(target)]
    second = (block_of(target) + shards_of // 2) % shards_of
    return jnp.where((block_of(source) == first) | (block_of(source) == second), factor * values, values)


def block_scale(stream_key, dims, cuts, low, largest):
    gain = 1.0
    for axis_at, blocks in cuts:
        draws = jax.random.uniform(jax.random.fold_in(jax.random.fold_in(stream_key, 6), axis_at), (blocks,), jnp.float32, low / len(cuts), largest / len(cuts))
        gain = gain * jnp.repeat(jnp.exp(draws), dims[axis_at] // blocks).reshape((-1,) + (1,) * (len(dims) - 1 - axis_at))
    return gain


def bell_draw(rng, shape, scale, most, cuts=(), kind=jnp.bfloat16):
    values = jax.random.normal(rng, shape, jnp.float32) * scale
    if len(cuts) > 0:
        values = block_scale(rng, shape, cuts, -0.22, 0.18) * values
    return jnp.clip(values, min=-most, max=most).astype(kind)


def noise_with(own_key, dims, scale, most, cuts, heavy, kind=jnp.bfloat16):
    values = scale * jax.random.normal(own_key, dims, jnp.float32)
    if cuts:
        values = values * block_scale(own_key, dims, cuts, -0.22, 0.18)
    return jnp.clip(raised(values, jax.random.fold_in(own_key, 3), *heavy), -most, most).astype(kind)


def setup_inputs(seed: int = 0) -> dict:
    key_list = jax.random.split(jax.random.key(seed), 16)
    block_in = bell_draw(key_list[0], (ROWS, ROW_LEN, D), 1.0, 6.0, ((0, 4), (1, 8)))
    cotangent = noise_with(key_list[1], (ROWS, ROW_LEN, D), 1.0, 6.0, ((0, 4), (1, 8)), (0, 2, 4, 2.0))
    seg_lengths = draw_seg_lengths(jax.random.fold_in(key_list[15], 71), 0)
    ln1_gain = jnp.clip(1.0 + 0.1 * jax.random.normal(key_list[3], (D,), jnp.float32), 0.5, 1.5).astype(jnp.bfloat16)
    ln1_bias = bell_draw(key_list[4], (D,), 0.3, 1.5)
    qkv_weight = bell_draw(key_list[5], (D, 3 * D), D ** -0.5, 0.125, ((0, 4),))
    qkv_bias = bell_draw(key_list[6], (3 * D,), 0.3, 1.5)
    out_weight = bell_draw(key_list[7], (D, D), (max(D // 64, 16)) ** -0.5, 1.0, ((0, 4),))
    out_bias = bell_draw(key_list[8], (D,), 0.3, 1.5)
    ln2_gain = jnp.clip(1.0 + 0.1 * jax.random.normal(key_list[9], (D,), jnp.float32), 0.5, 1.5).astype(jnp.bfloat16)
    ln2_bias = bell_draw(key_list[10], (D,), 0.3, 1.5)
    fc1_weight = bell_draw(key_list[11], (D, FF), D ** -0.5, 0.125, ((0, 4),))
    fc1_bias = bell_draw(key_list[12], (FF,), 0.3, 1.5)
    fc2_weight = bell_draw(key_list[13], (D, FF), FF ** -0.5, 0.0625, ((0, 4),))
    fc2_bias = bell_draw(key_list[14], (D,), 0.3, 1.5)
    return dict(block_in=block_in, cotangent=cotangent, seg_lengths=seg_lengths, ln1_gain=ln1_gain, ln1_bias=ln1_bias, qkv_weight=qkv_weight, qkv_bias=qkv_bias, out_weight=out_weight, out_bias=out_bias, ln2_gain=ln2_gain, ln2_bias=ln2_bias, fc1_weight=fc1_weight, fc1_bias=fc1_bias, fc2_weight=fc2_weight, fc2_bias=fc2_bias)


NORM_EPS = 1e-05
NEG_FILL = -1e+30
ROT_BASE = 10000.0
HIGHEST = lax.Precision.HIGHEST

@jax.custom_vjp
def low(v):
    return lax.optimization_barrier(v.astype(jnp.bfloat16)).astype(jnp.float32)

@jax.custom_vjp
def low_back(v):
    return v

def low_keep(v):
    return (low(v), None)

def low_pass(kept, grad):
    return (grad,)

def back_keep(v):
    return (v, None)

def back_low(kept, grad):
    return (low(grad),)
low.defvjp(low_keep, low_pass)
low_back.defvjp(back_keep, back_low)

def layer_norm(inputs, gain_vec, bias_vec):
    centred = inputs - lax.optimization_barrier(jnp.mean(inputs, axis=-1, keepdims=True))
    spread = lax.optimization_barrier(jnp.mean(centred * centred, axis=-1, keepdims=True))
    return centred * lax.rsqrt(spread + NORM_EPS) * gain_vec + bias_vec

def segment_info(lengths, places):
    seg_ends = jnp.cumsum(lengths, axis=-1).astype(jnp.int32)
    passed = (places[..., :, None] >= seg_ends[..., None, :]).astype(jnp.int32)
    segment = lax.optimization_barrier(jnp.sum(passed, axis=-1)).astype(jnp.int32)
    seg_start = lax.optimization_barrier(jnp.sum(passed * lengths[..., None, :], axis=-1)).astype(jnp.int32)
    return (segment, (places - seg_start).astype(jnp.int32))

def rotate(values, places, direction):
    half_rot = ROT // 2
    frequency = ROT_BASE ** (-(2.0 * jnp.arange(half_rot, dtype=jnp.float32)) / ROT)
    angles = places.astype(jnp.float32)[..., None] * frequency
    cosine = jnp.cos(angles)[..., None, :]
    sine_part = direction * jnp.sin(angles)[..., None, :]
    lower_half = values[..., :half_rot]
    upper_half = values[..., half_rot:ROT]
    return jnp.concatenate([lower_half * cosine - upper_half * sine_part, upper_half * cosine + lower_half * sine_part, values[..., ROT:]], axis=-1)

def row_block(weights, row_in, row_lengths):
    gain_one, bias_one, qkv_w, qkv_b, out_w, out_b, gain_two, bias_two, fc1_w, fc1_b, fc2_w, fc2_b = weights
    length = row_in.shape[0]
    places = jnp.arange(length, dtype=jnp.int32)
    segment, offset = segment_info(row_lengths, places)
    attn_in = low(layer_norm(row_in, gain_one, bias_one))
    joined = low_back(jnp.dot(attn_in, qkv_w, precision=HIGHEST) + qkv_b).reshape(length, 3, HEADS, HEAD_SIZE)
    query = low(low_back(rotate(joined[:, 0], offset, 1.0)))
    keyed = low(low_back(rotate(joined[:, 1], offset, 1.0)))
    valued = low(low_back(joined[:, 2]))
    scores = low_back(jnp.einsum('qhd,khd->hqk', query, keyed, precision=HIGHEST) * HEAD_SIZE ** (-0.5))
    allowed = (segment[:, None] == segment[None, :]) & (places[None, :] <= places[:, None])
    scores = jnp.where(allowed[None], scores, NEG_FILL)
    probs_low = low(jax.nn.softmax(scores, axis=-1))
    context = low(low_back(jnp.einsum('hqk,khd->qhd', probs_low, valued, precision=HIGHEST)))
    context = context.reshape(length, HEADS * HEAD_SIZE)
    attn_out = jnp.dot(context, out_w, precision=HIGHEST) + out_b
    mlp_in = low(layer_norm(row_in, gain_two, bias_two))
    hidden = low_back(jnp.dot(mlp_in, fc1_w, precision=HIGHEST) + fc1_b)
    active = low(jax.nn.gelu(hidden, approximate=False))
    mlp_out = jnp.dot(active, fc2_w.T, precision=HIGHEST) + fc2_b
    squares = jnp.stack([jnp.sum(attn_out * attn_out), jnp.sum(mlp_out * mlp_out)])
    return (row_in + attn_out + mlp_out, squares)

def reference(block_in, cotangent, seg_lengths, ln1_gain, ln1_bias, qkv_weight, qkv_bias, out_weight, out_bias, ln2_gain, ln2_bias, fc1_weight, fc1_bias, fc2_weight, fc2_bias):
    weights = tuple((element.astype(jnp.float32) for element in (ln1_gain, ln1_bias, qkv_weight, qkv_bias, out_weight, out_bias, ln2_gain, ln2_bias, fc1_weight, fc1_bias, fc2_weight, fc2_bias)))
    inputs = block_in.astype(jnp.float32)

    def forward(params, rows_in):

        def one_row(row_pair):
            return jax.checkpoint(row_block)(params, row_pair[0], row_pair[1])
        return lax.map(one_row, (rows_in, seg_lengths.astype(jnp.int32)))
    outputs, pullback, squares = jax.vjp(forward, weights, inputs, has_aux=True)
    weight_grads, input_grad = pullback(cotangent.astype(jnp.float32))
    entries = outputs.size
    totals = lax.optimization_barrier(jnp.sum(squares, axis=0))
    branch_rms = jnp.sqrt(totals / entries)
    return (outputs.astype(jnp.bfloat16), input_grad.astype(jnp.bfloat16), weight_grads[0], weight_grads[1], weight_grads[2], weight_grads[3], weight_grads[4], weight_grads[5], weight_grads[6], weight_grads[7], weight_grads[8], weight_grads[9], weight_grads[10], weight_grads[11], branch_rms[0], branch_rms[1])
```

```python
import functools

import jax
import jax.numpy as jnp
from jax import lax
from jax.experimental import pallas as pl
from jax.experimental.pallas import tpu as pltpu
from jax.sharding import PartitionSpec as P

HEADS = 8
HEAD_SIZE = 256
ROT = 64
NORM_EPS = 1e-05
NEG_FILL = -1e30
ROT_BASE = 10000.0
BF = jnp.bfloat16
F32 = jnp.float32


def across(values, offset):
    count = lax.axis_size("head")
    return lax.ppermute(values, "head", [(i, i ^ offset) for i in range(count)])


def other_core(values):
    return lax.ppermute(values, "blk", [(0, 1), (1, 0)])


def plane_gather(own):
    half = own.shape[0] // 2
    one = across(own, 1)
    two = across(own, 2)
    three = jnp.concatenate([across(one[:half], 2), across(two[half:], 1)], axis=0)
    near = [own, one, two, three]
    return near + [other_core(piece) for piece in near]


def plane_scatter(partial, span):
    count = lax.axis_size("head")
    width = partial.shape[1]
    side = width // 2
    near = count * span
    got = other_core(partial[near:])
    mine = (partial[:near].astype(F32) + got.astype(F32)).reshape(count, span, width)
    left, right = mine[:, :, :side], mine[:, :, side:]
    left_got = across(jnp.stack([left[1], left[3]]).astype(BF), 1).astype(F32)
    right_got = across(jnp.stack([right[2], right[3]]).astype(BF), 2).astype(F32)
    left_last = across((left[2] + left_got[1]).astype(BF), 2).astype(F32)
    right_last = across((right[1] + right_got[1]).astype(BF), 1).astype(F32)
    return jnp.concatenate(
        [left[0] + left_got[0] + left_last, right[0] + right_got[0] + right_last], axis=1
    )


def data_gather(own):
    count = lax.axis_size("dp")
    place = lax.axis_index("dp")
    rows = own.shape[0]
    up = down = own
    ups, downs = [], []
    for step in range(1, count):
        up = lax.ppermute(up, "dp", [(i, i + 1) for i in range(step - 1, count - 1)])
        down = lax.ppermute(down, "dp", [(i + 1, i) for i in range(count - step)])
        ups.append(up)
        downs.append(down)
    whole = jnp.zeros((count * rows,) + own.shape[1:], own.dtype)
    whole = lax.dynamic_update_slice_in_dim(whole, own, place * rows, 0)
    for step in range(1, count):
        piece = jnp.where(place + step < count, downs[step - 1], ups[count - step - 1])
        source = lax.rem(place + step, count)
        whole = lax.dynamic_update_slice_in_dim(whole, piece, source * rows, 0)
    return whole


def data_scatter(partial):
    count = lax.axis_size("dp")
    place = lax.axis_index("dp")
    rows = partial.shape[0] // count

    def chunk(offset):
        at = jnp.clip(place + offset, 0, count - 1)
        return lax.dynamic_slice_in_dim(partial, at * rows, rows, 0)

    up = chunk(count - 1)
    down = chunk(1 - count)
    for step in range(count - 1, 0, -1):
        up = lax.ppermute(up.astype(BF), "dp", [(i, i + 1) for i in range(count - step)])
        down = lax.ppermute(
            down.astype(BF), "dp", [(i + 1, i) for i in range(step - 1, count - 1)]
        )
        if step > 1:
            up = up.astype(F32) + chunk(step - 1).astype(F32)
            down = down.astype(F32) + chunk(1 - step).astype(F32)
    return chunk(0).astype(F32) + up.astype(F32) + down.astype(F32)


def spread_columns(piece, places, parts):
    rows, width = piece.shape
    each = width // parts
    pieces = plane_gather(piece)
    total = len(pieces)
    whole = jnp.zeros((rows, parts * total * each), F32)
    for relative, block in enumerate(pieces):
        for part in range(parts):
            whole = lax.dynamic_update_slice(
                whole,
                block[:, part * each : (part + 1) * each].astype(F32),
                (0, (part * total + places[relative]) * each),
            )
    return whole


def turn(values, cosine, sine):
    low = values[:, : cosine.shape[1]]
    lane = lax.broadcasted_iota(jnp.int32, low.shape, 1)
    half = ROT // 2
    partner = jnp.where(
        lane < half, pltpu.roll(low, low.shape[1] - half, 1), pltpu.roll(low, half, 1)
    )
    return jnp.concatenate([low * cosine + partner * sine, values[:, cosine.shape[1] :]], axis=1)


def attention_kernel(
    order, first, qkv, bias, upstream, cosine, sine, context, context_rel, grads, keys, values,
    score, prob_grad, key_sum, value_sum,
):
    step = pl.program_id(0)
    total = pl.num_programs(0)
    size = HEAD_SIZE
    span = qkv.shape[1]
    last = (((1,), (1,)), ((), ()))
    rows = (((0,), (0,)), ((), ()))
    mine = order[step]
    start = first[step]
    cos_here, sin_here = cosine[mine], sine[mine]
    joined = qkv[0] + bias[...]
    query = (turn(joined[:, :size], cos_here, sin_here) * (size**-0.5)).astype(BF)
    at = pl.ds(pl.multiple_of(step * span, span), span)
    keys[at, :] = turn(joined[:, size : 2 * size], cos_here, sin_here).astype(BF)
    values[at, :] = joined[:, 2 * size :].astype(BF)
    key_sum[at, :] = jnp.zeros((span, size), F32)
    value_sum[at, :] = jnp.zeros((span, size), F32)
    up = upstream[0]

    def one(count):
        blocks = [slice(i * span, (i + 1) * span) for i in range(count)]
        top = jnp.full((span, 1), NEG_FILL, F32)
        for i, block in enumerate(blocks):
            part = lax.dot_general(query, keys[block, :], last, preferred_element_type=F32)
            if i == count - 1:
                row = lax.broadcasted_iota(jnp.int32, part.shape, 0)
                column = lax.broadcasted_iota(jnp.int32, part.shape, 1)
                part = jnp.where(column <= row, part, NEG_FILL)
            else:
                part = part + jnp.where(i >= start, 0.0, NEG_FILL)
            score[:, block] = part
            top = jnp.maximum(top, jnp.max(part, axis=1, keepdims=True))
        norm = jnp.zeros((span, 1), F32)
        for block in blocks:
            part = jnp.exp(score[:, block] - top)
            score[:, block] = part
            norm = norm + jnp.sum(part, axis=1, keepdims=True)
        inverse = 1.0 / norm
        out = jnp.zeros((span, size), F32)
        inner = jnp.zeros((span, 1), F32)
        for block in blocks:
            probs = score[:, block] * inverse
            score[:, block] = probs
            grad = lax.dot_general(up, values[block, :], last, preferred_element_type=F32)
            prob_grad[:, block] = grad
            inner = inner + jnp.sum(probs * grad, axis=1, keepdims=True)
            low = probs.astype(BF)
            out = out + jnp.dot(low, values[block, :], preferred_element_type=F32)
            value_sum[block, :] += lax.dot_general(low, up, rows, preferred_element_type=F32)
        context[0] = out.astype(BF)
        context_rel[0] = out.astype(BF)
        query_grad = jnp.zeros((span, size), F32)
        for block in blocks:
            low = (score[:, block] * (prob_grad[:, block] - inner)).astype(BF)
            query_grad = query_grad + jnp.dot(low, keys[block, :], preferred_element_type=F32)
            key_sum[block, :] += lax.dot_general(low, query, rows, preferred_element_type=F32)
        query_grad = (query_grad * (size**-0.5)).astype(BF).astype(F32)
        grads[mine, :, :size] = turn(query_grad, cos_here, -sin_here).astype(BF)

    steps = keys.shape[0] // span
    for index in range(steps):
        pl.when(step == index)(functools.partial(one, index + 1))

    @pl.when(step == total - 1)
    def finish():
        def each(index, carry):
            place = order[index]
            block = pl.ds(pl.multiple_of(index * span, span), span)
            key_grad = key_sum[block, :].astype(BF).astype(F32)
            grads[place, :, size : 2 * size] = turn(key_grad, cosine[place], -sine[place]).astype(
                BF
            )
            grads[place, :, 2 * size :] = value_sum[block, :].astype(BF)
            return carry

        lax.fori_loop(0, total, each, 0)


def attention(order, first, qkv, bias, upstream, cosine, sine):
    count, span, width = qkv.shape
    size = HEAD_SIZE
    length = count * span
    whole = lambda *shape: pl.BlockSpec(shape, lambda i, o, f: (0,) * len(shape))
    taken = lambda *shape: pl.BlockSpec(
        (1,) + shape, lambda i, o, f: (o[i],) + (0,) * len(shape)
    )
    pairs = count * (count + 1) // 2
    return pl.pallas_call(
        attention_kernel,
        grid_spec=pltpu.PrefetchScalarGridSpec(
            num_scalar_prefetch=2,
            grid=(count,),
            in_specs=[
                taken(span, width),
                whole(1, width),
                taken(span, size),
                whole(count, span, cosine.shape[-1]),
                whole(count, span, cosine.shape[-1]),
            ],
            out_specs=[
                pl.BlockSpec((1, span, size), lambda i, o, f: (i, 0, 0)),
                taken(span, size),
                whole(count, span, width),
            ],
            scratch_shapes=[
                pltpu.VMEM((length, size), BF),
                pltpu.VMEM((length, size), BF),
                pltpu.VMEM((span, length), F32),
                pltpu.VMEM((span, length), F32),
                pltpu.VMEM((length, size), F32),
                pltpu.VMEM((length, size), F32),
            ],
        ),
        out_shape=[
            jax.ShapeDtypeStruct((count, span, size), BF),
            jax.ShapeDtypeStruct((count, span, size), BF),
            jax.ShapeDtypeStruct((count, span, width), BF),
        ],
        compiler_params=pltpu.CompilerParams(vmem_limit_bytes=40 * 2**20),
        cost_estimate=pl.CostEstimate(
            flops=pairs * span * span * size * 12 * 2,
            bytes_accessed=length * (width * 6 + size * 6 + 1024),
            transcendentals=pairs * span * span,
        ),
        name="attention",
    )(order, first, qkv, bias, upstream, cosine, sine)


def body(
    block_in,
    cotangent,
    seg_lengths,
    ln1_gain,
    ln1_bias,
    qkv_weight,
    qkv_bias,
    out_weight,
    out_bias,
    ln2_gain,
    ln2_bias,
    fc1_weight,
    fc1_bias,
    fc2_weight,
    fc2_bias,
):
    rows_here, span, width = block_in.shape
    shard, hidden_units = fc1_weight.shape
    data_count = lax.axis_size("dp")
    head_count = lax.axis_size("head")
    blk_count = lax.axis_size("blk")
    plane = head_count * blk_count
    head_place = lax.axis_index("head")
    blk_place = lax.axis_index("blk")
    place = head_place * blk_count + blk_place
    contract_last = (((1,), (1,)), ((), ()))
    contract = (((0,), (0,)), ((), ()))
    each = hidden_units // plane
    length = plane * span

    places = [
        (head_place ^ (r % head_count)) * blk_count + (blk_place ^ (r // head_count))
        for r in range(plane)
    ]
    absolute = jnp.arange(plane, dtype=jnp.int32)
    order = (absolute % blk_count ^ blk_place) * head_count + (absolute // blk_count ^ head_place)

    def columns(values, wide):
        return lax.dynamic_slice_in_dim(values, place * wide, wide, 1)

    out_mine = data_gather(columns(out_weight, HEAD_SIZE))
    qkv_mine = data_gather(
        jnp.concatenate(
            [
                columns(qkv_weight[:, part * width : (part + 1) * width], HEAD_SIZE)
                for part in range(3)
            ],
            axis=1,
        )
    )
    fc1_mine = data_gather(columns(fc1_weight, each))
    fc2_mine = data_gather(columns(fc2_weight, each))
    own_in = block_in.reshape(span, width)
    own_up = cotangent.reshape(span, width)
    tokens = jnp.concatenate(plane_gather(own_in), axis=0)
    upstream = jnp.concatenate(plane_gather(own_up), axis=0)

    lengths = seg_lengths.reshape(-1)
    starts = jnp.stack([jnp.sum(lengths[:i]) for i in range(lengths.shape[0])])
    block_at = absolute * span
    block_start = jnp.max(
        jnp.where(starts[None, :] <= block_at[:, None], starts[None, :], 0), axis=1
    ).astype(jnp.int32)
    first = block_start // span
    relative_at = jnp.stack(places)
    seg_at = jnp.max(
        jnp.where(starts[None, :] <= relative_at[:, None] * span, starts[None, :], 0), axis=1
    )
    offset = (relative_at * span - seg_at)[:, None] + jnp.arange(span, dtype=jnp.int32)[None, :]
    half = ROT // 2
    frequency = ROT_BASE ** (-(2.0 * jnp.arange(half, dtype=F32)) / ROT)
    angles = offset.astype(F32)[..., None] * frequency
    cosine, sine = jnp.cos(angles), jnp.sin(angles)
    rest = jnp.zeros((plane, span, 128 - ROT), F32)
    cosine = jnp.concatenate([cosine, cosine, rest + 1.0], axis=-1)
    sine = jnp.concatenate([-sine, sine, rest], axis=-1)

    inputs = tokens.astype(F32)
    centred = inputs - jnp.mean(inputs, axis=-1, keepdims=True)
    scaled = lax.rsqrt(jnp.mean(centred * centred, axis=-1, keepdims=True) + NORM_EPS)
    normed = centred * scaled
    attn_in = (normed * ln1_gain + ln1_bias).astype(BF)
    mlp_in = (normed * ln2_gain + ln2_bias).astype(BF)

    out_pieces = plane_gather(out_mine)
    out_full = jnp.zeros((width, width), BF)
    for relative, block in enumerate(out_pieces):
        out_full = lax.dynamic_update_slice(
            out_full, block, (0, places[relative] * HEAD_SIZE)
        )
    out_rows = lax.dynamic_slice_in_dim(out_full, place * HEAD_SIZE, HEAD_SIZE, 0)
    context_grad = lax.dot_general(
        upstream, out_rows, contract_last, preferred_element_type=F32
    ).astype(BF)
    joined = jnp.dot(attn_in, qkv_mine, preferred_element_type=F32)
    bias_mine = jnp.concatenate(
        [
            lax.dynamic_slice_in_dim(qkv_bias, part * width + place * HEAD_SIZE, HEAD_SIZE, 0)
            for part in range(3)
        ]
    ).astype(F32)
    context_abs, context, qkv_grad = attention(
        order.astype(jnp.int32),
        first,
        joined.reshape(plane, span, 3 * HEAD_SIZE),
        bias_mine[None, :],
        context_grad.reshape(plane, span, HEAD_SIZE),
        cosine,
        sine,
    )
    context = context.reshape(length, HEAD_SIZE)
    qkv_grad = qkv_grad.reshape(length, 3 * HEAD_SIZE)
    own_context = lax.all_to_all(
        context_abs.reshape(length, HEAD_SIZE),
        ("head", "blk"),
        split_axis=0,
        concat_axis=1,
        tiled=True,
    )
    attn_out = jnp.dot(own_context, out_full, preferred_element_type=F32) + out_bias
    out_grad = lax.dot_general(context, upstream, contract, preferred_element_type=F32).astype(BF)
    out_grad = lax.all_to_all(out_grad, ("head", "blk"), split_axis=1, concat_axis=0, tiled=True)
    qkv_w_grad = lax.dot_general(attn_in, qkv_grad, contract, preferred_element_type=F32).astype(BF)
    attn_in_grad = lax.dot_general(
        qkv_grad, qkv_mine, contract_last, preferred_element_type=F32
    )

    hidden = jnp.dot(mlp_in, fc1_mine, preferred_element_type=F32)
    hidden = hidden + lax.dynamic_slice_in_dim(fc1_bias, place * each, each, 0)
    phi = 0.5 * (1.0 + lax.erf(hidden * (0.5**0.5)))
    active = (hidden * phi).astype(BF)
    slope = phi + hidden * jnp.exp(-0.5 * hidden * hidden) * ((2.0 * jnp.pi) ** -0.5)
    fc2_grad = lax.dot_general(upstream, active, contract, preferred_element_type=F32).astype(BF)
    mlp_part = lax.dot_general(
        active, fc2_mine, contract_last, preferred_element_type=F32
    ).astype(BF)
    hidden_grad = (jnp.dot(upstream, fc2_mine, preferred_element_type=F32) * slope).astype(BF)
    fc1_grad = lax.dot_general(mlp_in, hidden_grad, contract, preferred_element_type=F32).astype(BF)
    mlp_in_grad = lax.dot_general(
        hidden_grad, fc1_mine, contract_last, preferred_element_type=F32
    )

    mlp_out = plane_scatter(mlp_part, span) + fc2_bias
    own_float = own_in.astype(F32)
    block_out = (own_float + attn_out + mlp_out).astype(BF).reshape(block_in.shape)

    share_part = (attn_in_grad * ln1_gain + mlp_in_grad * ln2_gain).astype(BF)
    share = plane_scatter(share_part, span)
    own_centred = own_float - jnp.mean(own_float, axis=-1, keepdims=True)
    own_scaled = lax.rsqrt(jnp.mean(own_centred * own_centred, axis=-1, keepdims=True) + NORM_EPS)
    own_normed = own_centred * own_scaled
    share = own_scaled * (
        share
        - jnp.mean(share, axis=-1, keepdims=True)
        - own_normed * jnp.mean(share * own_normed, axis=-1, keepdims=True)
    )
    input_grad = (own_up.astype(F32) + share).astype(BF).reshape(block_in.shape)

    fc2_out = spread_columns(data_scatter(fc2_grad).astype(BF), places, 1)
    fc1_out = spread_columns(data_scatter(fc1_grad).astype(BF), places, 1)
    out_out = spread_columns(data_scatter(out_grad).astype(BF), places, 1)
    qkv_out = spread_columns(data_scatter(qkv_w_grad).astype(BF), places, 3)

    qkv_bias_part = jnp.sum(qkv_grad.astype(F32), axis=0).reshape(3, 1, HEAD_SIZE)
    here = (jnp.arange(plane) == place).astype(F32)
    qkv_bias_part = (qkv_bias_part * here[None, :, None]).reshape(-1)
    fc1_bias_part = (
        here[:, None] * jnp.sum(hidden_grad.astype(F32), axis=0)[None, :]
    ).reshape(-1)
    reduced = lax.psum(
        (
            jnp.sum(attn_in_grad * normed, axis=0),
            jnp.sum(attn_in_grad, axis=0),
            qkv_bias_part,
            jnp.sum(own_up.astype(F32), axis=0),
            jnp.sum(mlp_in_grad * normed, axis=0),
            jnp.sum(mlp_in_grad, axis=0),
            fc1_bias_part,
            jnp.stack([jnp.sum(attn_out * attn_out), jnp.sum(mlp_out * mlp_out)]),
        ),
        ("dp", "head", "blk"),
    )
    entries = rows_here * length * data_count * width
    branch_rms = jnp.sqrt(reduced[7] / entries)
    return (
        block_out,
        input_grad,
        reduced[0],
        reduced[1],
        qkv_out,
        reduced[2],
        out_out,
        reduced[3],
        reduced[4],
        reduced[5],
        fc1_out,
        reduced[6],
        fc2_out,
        reduced[3],
        branch_rms[0],
        branch_rms[1],
    )


def solution(mesh):
    rows, tokens, whole = P("dp", None), P("dp", ("head", "blk"), None), P()
    return jax.shard_map(
        body,
        mesh=mesh,
        in_specs=(
            tokens,
            tokens,
            rows,
            whole,
            whole,
            rows,
            whole,
            rows,
            whole,
            whole,
            whole,
            rows,
            whole,
            rows,
            whole,
        ),
        out_specs=(
            tokens,
            tokens,
            whole,
            whole,
            rows,
            whole,
            rows,
            whole,
            whole,
            whole,
            rows,
            whole,
            rows,
            whole,
            whole,
            whole,
        ),
        check_vma=False,
    )
```

```python
import functools

import jax
import jax.numpy as jnp
from jax import lax
from jax.experimental import pallas as pl
from jax.experimental.pallas import tpu as pltpu
from jax.sharding import PartitionSpec as P

HEADS = 8
HEAD_SIZE = 256
ROT = 64
NORM_EPS = 1e-05
NEG_FILL = -1e30
ROT_BASE = 10000.0
BF = jnp.bfloat16
F32 = jnp.float32
NN = (((1,), (0,)), ((), ()))
NT = (((1,), (1,)), ((), ()))
TN = (((0,), (0,)), ((), ()))
LIGHT = pl.CostEstimate(flops=10**9, bytes_accessed=10**6, transcendentals=0)
ROOM = pltpu.CompilerParams(vmem_limit_bytes=48 * 2**20)
MORE_ROOM = pltpu.CompilerParams(vmem_limit_bytes=48 * 2**20)


def across(values, offset):
    count = lax.axis_size("head")
    return lax.ppermute(values, "head", [(i, i ^ offset) for i in range(count)])


def other_core(values):
    return lax.ppermute(values, "blk", [(0, 1), (1, 0)])


def tie(*trees):
    leaves, form = jax.tree.flatten(trees)
    return jax.tree.unflatten(form, lax.optimization_barrier(leaves))


def gather_start(own):
    return own, across(own, 1), across(own, 2)


def gather_middle(own, one, two):
    half = own.shape[0] // 2
    return own, one, two, across(one[:half], 2), across(two[half:], 1)


def gather_end(*pieces):
    near = jnp.concatenate(pieces, axis=0)
    return near, other_core(near)


def data_gather(own):
    return lax.all_gather(own, "dp", axis=0, tiled=True)


def data_scatter(partial):
    return lax.psum_scatter(partial, "dp", scatter_dimension=0, tiled=True)


def hop_up(values):
    return lax.ppermute(values, "dp", [(0, 1), (1, 2), (2, 3)])


def hop_down(values):
    return lax.ppermute(values, "dp", [(3, 2), (2, 1), (1, 0)])


def part_of(sums, index):
    rows = sums.shape[0] // 4
    return lax.dynamic_slice_in_dim(sums, index * rows, rows, 0)


def exchange_one(own, sums):
    place = lax.axis_index("dp")
    return (
        hop_up(jnp.where(place == 0, part_of(sums, 3), own)),
        hop_down(jnp.where(place == 3, part_of(sums, 0), own)),
    )


def exchange_two(own, sums, up, down):
    place = lax.axis_index("dp")
    up = jnp.where(place == 0, own, jnp.where(place == 1, plus(part_of(sums, 3), up), up))
    down = jnp.where(place == 3, own, jnp.where(place == 2, plus(part_of(sums, 0), down), down))
    return hop_up(up), hop_down(down)


def exchange_three(sums, up, down):
    place = lax.axis_index("dp")
    more_up = plus(part_of(sums, 3), up)
    more_down = plus(part_of(sums, 0), down)
    up = jnp.where(place == 0, part_of(sums, 2), jnp.where(place == 2, more_up, up))
    down = jnp.where(place == 3, part_of(sums, 1), jnp.where(place == 1, more_down, down))
    return hop_up(up), hop_down(down)


def exchange_four(sums, up, down):
    place = lax.axis_index("dp")
    more_up = plus(part_of(sums, 2), up)
    more_down = plus(part_of(sums, 1), down)
    up = jnp.where(place == 0, part_of(sums, 1), jnp.where(place == 1, more_up, up))
    down = jnp.where(place == 3, part_of(sums, 2), jnp.where(place == 2, more_down, down))
    return hop_up(up), hop_down(down)


def exchange_end(own, sums, one, two, three, four):
    place = lax.axis_index("dp")
    rows = own.shape[0]

    def choose(*values):
        out = values[-1]
        for index in range(len(values) - 2, -1, -1):
            if values[index] is not out:
                out = jnp.where(place == index, values[index], out)
        return out

    up, down = 0, 1
    whole = jnp.zeros((4 * rows,) + own.shape[1:], own.dtype)
    for step, piece in enumerate(
        (
            own,
            jnp.where(place < 2, one[down], choose(two[down], two[down], two[down], four[up])),
            choose(two[down], three[down], three[up], two[up]),
            jnp.where(place >= 2, one[up], choose(four[down], two[up], two[up], two[up])),
        )
    ):
        whole = lax.dynamic_update_slice_in_dim(whole, piece, (place + step) % 4 * rows, 0)
    first = choose(three[down], four[up], four[up], three[up]).astype(F32)
    inner = (place == 1) | (place == 2)
    second = jnp.where(inner, four[down].astype(F32), 0.0)
    total = part_of(sums, place).astype(F32) + first + second
    return whole, total.astype(BF)


def plus(one, two):
    return (one.astype(F32) + two.astype(F32)).astype(BF)


def sum_moves():
    moves = []
    for axis in ("blk", "head", "dp"):
        count = lax.axis_size(axis)
        moves += [
            (axis, [(i, i ^ 2**k) for i in range(count)]) for k in range(count.bit_length() - 1)
        ]
    return moves


def sum_move(vector, move):
    return vector + lax.ppermute(vector, *move)


def whole(array):
    return pl.BlockSpec(array.shape, lambda i: (0,) * array.ndim)


def product(one, two, dims, tile=512, kind=BF):
    def kernel(left, right, out):
        out[...] = lax.dot_general(
            left[...], right[...], dims, preferred_element_type=F32
        ).astype(out.dtype)

    if dims == TN:
        rows, left_spec = one.shape[1], pl.BlockSpec((one.shape[0], tile), lambda i: (0, i))
    else:
        rows, left_spec = one.shape[0], pl.BlockSpec((tile, one.shape[1]), lambda i: (i, 0))
    columns = two.shape[0] if dims == NT else two.shape[1]
    return pl.pallas_call(
        kernel,
        grid=(rows // tile,),
        in_specs=[left_spec, whole(two)],
        out_specs=pl.BlockSpec((tile, columns), lambda i: (i, 0)),
        out_shape=jax.ShapeDtypeStruct((rows, columns), kind),
        compiler_params=ROOM,
        cost_estimate=LIGHT,
        name="product",
    )(one, two)


def wide_product(one, two, tile=512):
    def kernel(left, right, out):
        out[...] = lax.dot_general(
            left[...], right[...], TN, preferred_element_type=F32
        ).astype(BF)

    return pl.pallas_call(
        kernel,
        grid=(two.shape[1] // tile,),
        in_specs=[whole(one), pl.BlockSpec((two.shape[0], tile), lambda i: (0, i))],
        out_specs=pl.BlockSpec((one.shape[1], tile), lambda i: (0, i)),
        out_shape=jax.ShapeDtypeStruct((one.shape[1], two.shape[1]), BF),
        compiler_params=ROOM,
        cost_estimate=LIGHT,
        name="wide",
    )(one, two)


def hidden_kernel(tokens, weight, bias, active, slope):
    hidden = jnp.dot(tokens[...], weight[...], preferred_element_type=F32) + bias[...]
    phi = 0.5 * (1.0 + lax.erf(hidden * (0.5**0.5)))
    active[...] = (hidden * phi).astype(BF)
    density = jnp.exp(-0.5 * hidden * hidden) * ((2.0 * jnp.pi) ** -0.5)
    slope[...] = (phi + hidden * density).astype(BF)


def hidden_units_of(tokens, weight, bias, tile=512):
    rows, width = tokens.shape
    wide = weight.shape[1]
    out = pl.BlockSpec((tile, wide), lambda i: (i, 0))
    return pl.pallas_call(
        hidden_kernel,
        grid=(rows // tile,),
        in_specs=[pl.BlockSpec((tile, width), lambda i: (i, 0)), whole(weight), whole(bias)],
        out_specs=[out, out],
        out_shape=[jax.ShapeDtypeStruct((rows, wide), BF)] * 2,
        compiler_params=MORE_ROOM,
        cost_estimate=LIGHT,
        name="hidden",
    )(tokens, weight, bias)


def hidden_grad_kernel(upstream, weight, slope, grad, total):
    values = jnp.dot(upstream[...], weight[...], preferred_element_type=F32)
    low = (values * slope[...].astype(F32)).astype(BF)
    grad[...] = low

    @pl.when(pl.program_id(0) == 0)
    def clear():
        total[...] = jnp.zeros_like(total)

    total[...] += jnp.sum(low.astype(F32), axis=0, keepdims=True)


def hidden_grad_of(upstream, weight, slope, tile=512):
    rows, width = upstream.shape
    wide = weight.shape[1]
    out = pl.BlockSpec((tile, wide), lambda i: (i, 0))
    return pl.pallas_call(
        hidden_grad_kernel,
        grid=(rows // tile,),
        in_specs=[pl.BlockSpec((tile, width), lambda i: (i, 0)), whole(weight), out],
        out_specs=[out, pl.BlockSpec((1, wide), lambda i: (0, 0))],
        out_shape=[
            jax.ShapeDtypeStruct((rows, wide), BF),
            jax.ShapeDtypeStruct((1, wide), F32),
        ],
        compiler_params=MORE_ROOM,
        cost_estimate=LIGHT,
        name="hidden_grad",
    )(upstream, weight, slope)


def halves_product(one, two, tile=512):
    half = two.shape[1] // 2

    def kernel(left, right, low, high):
        values = lax.dot_general(left[...], right[...], TN, preferred_element_type=F32).astype(BF)
        low[...] = values[:, :half]
        high[...] = values[:, half:]

    rows = one.shape[1]
    out = pl.BlockSpec((tile, half), lambda i: (i, 0))
    return pl.pallas_call(
        kernel,
        grid=(rows // tile,),
        in_specs=[pl.BlockSpec((one.shape[0], tile), lambda i: (0, i)), whole(two)],
        out_specs=[out, out],
        out_shape=[jax.ShapeDtypeStruct((rows, half), BF)] * 2,
        compiler_params=ROOM,
        cost_estimate=LIGHT,
        name="halves_product",
    )(one, two)


def put_split(step, side, block, left_keep, left_send, right_keep, right_send):
    left, right = block[:, :side], block[:, side:]
    for index, out, at in ((0, left_keep, 0), (1, left_send, 0), (2, left_keep, 1), (3, left_send, 1)):

        @pl.when(step == index)
        def write_left(out=out, at=at):
            out[at] = left

    for index, out, at in ((0, right_keep, 0), (1, right_keep, 1), (2, right_send, 0), (3, right_send, 1)):

        @pl.when(step == index)
        def write_right(out=out, at=at):
            out[at] = right


def split_shapes(span, width):
    return [jax.ShapeDtypeStruct((2, span, width // 2), BF)] * 4


def split_specs(span, width):
    return [pl.BlockSpec((2, span, width // 2), lambda i: (0, 0, 0))] * 4


def collect_start(left_keep, left_send, right_keep, right_send):
    return across(left_send, 1), across(right_send, 2)


def collect_middle(parts, got):
    (left_keep, _, right_keep, _), (left, right) = parts, got
    left_last = across(plus(left_keep[1], left[1]), 2)
    right_last = across(plus(right_keep[1], right[1]), 1)
    return (left_keep[0], left[0], left_last), (right_keep[0], right[0], right_last)


def collect_end(*sides):
    return jnp.concatenate(
        [sum(term.astype(F32) for term in terms[1:]) + terms[0].astype(F32) for terms in sides],
        axis=1,
    )


def product_far(one, two, tile=512):
    rows = one.shape[0] // 2

    def kernel(left, right, out):
        out[...] = lax.dot_general(
            left[...], right[...], NT, preferred_element_type=F32
        ).astype(BF)

    return pl.pallas_call(
        kernel,
        grid=(rows // tile,),
        in_specs=[
            pl.BlockSpec((tile, one.shape[1]), lambda i: (i + rows // tile, 0)),
            whole(two),
        ],
        out_specs=pl.BlockSpec((tile, two.shape[0]), lambda i: (i, 0)),
        out_shape=jax.ShapeDtypeStruct((rows, two.shape[0]), BF),
        compiler_params=ROOM,
        cost_estimate=LIGHT,
        name="far",
    )(one, two)


def product_near(one, two, got, span):
    width = two.shape[0]

    def kernel(left, right, more, *outs):
        values = lax.dot_general(left[...], right[...], NT, preferred_element_type=F32)
        block = (values + more[...].astype(F32)).astype(BF)
        put_split(pl.program_id(0), width // 2, block, *outs)

    return pl.pallas_call(
        kernel,
        grid=(one.shape[0] // 2 // span,),
        in_specs=[
            pl.BlockSpec((span, one.shape[1]), lambda i: (i, 0)),
            whole(two),
            pl.BlockSpec((span, width), lambda i: (i, 0)),
        ],
        out_specs=split_specs(span, width),
        out_shape=split_shapes(span, width),
        compiler_params=MORE_ROOM,
        cost_estimate=LIGHT,
        name="near",
    )(one, two, got)


def share_kernel(near, qkv, qkv_weight, hidden, weight, gain_one, gain_two, normed, *rest):
    outs, sums = rest[-5:-1] if near else rest[:1], rest[-1]
    one = lax.dot_general(qkv[...], qkv_weight[...], NT, preferred_element_type=F32)
    two = lax.dot_general(hidden[...], weight[...], NT, preferred_element_type=F32)
    scaled = normed[...].astype(F32)

    @pl.when(pl.program_id(0) == 0)
    def clear():
        sums[...] = jnp.zeros_like(sums)

    for row, values in enumerate((one * scaled, one, two * scaled, two)):
        sums[row : row + 1, :] += jnp.sum(values, axis=0, keepdims=True)
    share = one * gain_one[...] + two * gain_two[...]
    if near:
        block = (share + rest[0][...].astype(F32)).astype(BF)
        put_split(pl.program_id(0), share.shape[1] // 2, block, *outs)
    else:
        outs[0][...] = share.astype(BF)


def shares(near, qkv, qkv_weight, hidden, weight, gains, normed, span, got=None):
    rows, width = normed.shape
    steps = rows // 2 // span
    offset = 0 if near else steps

    def rows_of(array):
        return pl.BlockSpec((span, array.shape[1]), lambda i: (i + offset, 0))

    extra = [got] if near else []
    block = pl.BlockSpec((span, width), lambda i: (i, 0))
    return pl.pallas_call(
        functools.partial(share_kernel, near),
        grid=(steps,),
        in_specs=[
            rows_of(qkv),
            whole(qkv_weight),
            rows_of(hidden),
            whole(weight),
            whole(gains[0]),
            whole(gains[1]),
            rows_of(normed),
        ]
        + [block] * len(extra),
        out_specs=(split_specs(span, width) if near else [block])
        + [pl.BlockSpec((8, width), lambda i: (0, 0))],
        out_shape=(
            split_shapes(span, width) if near else [jax.ShapeDtypeStruct((rows // 2, width), BF)]
        )
        + [jax.ShapeDtypeStruct((8, width), F32)],
        compiler_params=MORE_ROOM,
        cost_estimate=LIGHT,
        name="share_near" if near else "share_far",
    )(qkv, qkv_weight, hidden, weight, *gains, normed, *extra)


def norm_kernel(near, far, gain_one, bias_one, gain_two, bias_two, normed, attn_in, mlp_in):
    half = pl.num_programs(0) // 2

    def write(block):
        values = block[...].astype(F32)
        centred = values - jnp.mean(values, axis=1, keepdims=True)
        spread = jnp.mean(centred * centred, axis=1, keepdims=True)
        scaled = centred * lax.rsqrt(spread + NORM_EPS)
        normed[...] = scaled.astype(BF)
        attn_in[...] = (scaled * gain_one[...] + bias_one[...]).astype(BF)
        mlp_in[...] = (scaled * gain_two[...] + bias_two[...]).astype(BF)

    pl.when(pl.program_id(0) < half)(lambda: write(near))
    pl.when(pl.program_id(0) >= half)(lambda: write(far))


def norms(near, far, span, *vectors):
    rows, width = near.shape
    half = rows // span
    vector = pl.BlockSpec((1, width), lambda i: (0, 0))
    block = pl.BlockSpec((span, width), lambda i: (i, 0))
    return pl.pallas_call(
        norm_kernel,
        grid=(2 * half,),
        in_specs=[
            pl.BlockSpec((span, width), lambda i: (jnp.minimum(i, half - 1), 0)),
            pl.BlockSpec((span, width), lambda i: (jnp.maximum(i - half, 0), 0)),
        ]
        + [vector] * 4,
        out_specs=[block] * 3,
        out_shape=[jax.ShapeDtypeStruct((2 * rows, width), BF)] * 3,
        compiler_params=ROOM,
        cost_estimate=LIGHT,
        name="norms",
    )(near, far, *[v.astype(F32)[None, :] for v in vectors])


def spread_kernel(parts, places, near, far, *outs):
    count = near.shape[0]
    each = near.shape[2] // sum(parts)
    for relative in range(2 * count):
        source = near if relative < count else far
        at = 0
        for out, part in zip(outs, parts):
            for index in range(part):
                where = (index * 2 * count + places[relative]) * each
                out[:, pl.ds(pl.multiple_of(where, each), each)] = source[
                    relative % count, :, at * each : (at + 1) * each
                ].astype(F32)
                at += 1


def spread_columns(near, far, places, parts):
    count = lax.axis_size("head")
    rows = near.shape[0] // count
    width = near.shape[1]
    step = min(rows, 64)
    each = width // sum(parts)
    taken = pl.BlockSpec((count, step, width), lambda i, p: (0, i, 0))
    wide = [2 * count * each * part for part in parts]
    return pl.pallas_call(
        functools.partial(spread_kernel, parts),
        grid_spec=pltpu.PrefetchScalarGridSpec(
            num_scalar_prefetch=1,
            grid=(rows // step,),
            in_specs=[taken, taken],
            out_specs=[pl.BlockSpec((step, w), lambda i, p: (i, 0)) for w in wide],
        ),
        out_shape=[jax.ShapeDtypeStruct((rows, w), F32) for w in wide],
        compiler_params=ROOM,
        cost_estimate=LIGHT,
        name="spread",
    )(places, near.reshape(count, rows, width), far.reshape(count, rows, width))


def halves_kernel(places, near, far, *rest):
    count = pl.num_programs(0) // 2
    out = rest[-1]

    def write(source):
        out[...] = source[...].astype(F32)

    pl.when(pl.program_id(0) < count)(lambda: write(near))
    pl.when(pl.program_id(0) >= count)(lambda: write(far))


def spread_half(near, far, places, side, first_column, begun=None):
    count = lax.axis_size("head")
    rows = near.shape[0] // count
    width = near.shape[1] - first_column
    column = first_column // width
    specs = [
        pl.BlockSpec((rows, width), lambda r, p: (jnp.minimum(r, count - 1), column)),
        pl.BlockSpec((rows, width), lambda r, p: (jnp.maximum(r - count, 0), column)),
    ]
    extra = () if begun is None else (begun,)
    return pl.pallas_call(
        halves_kernel,
        grid_spec=pltpu.PrefetchScalarGridSpec(
            num_scalar_prefetch=1,
            grid=(2 * count,),
            in_specs=specs + [pl.BlockSpec(memory_space=pl.ANY) for _ in extra],
            out_specs=pl.BlockSpec((rows, width), lambda r, p: (0, 2 * p[r] + side)),
        ),
        out_shape=jax.ShapeDtypeStruct((rows, 4 * count * width), F32),
        input_output_aliases={3: 0} if extra else {},
        compiler_params=ROOM,
        cost_estimate=LIGHT,
        name="halves",
    )(places, near, far, *extra)


def turn(values, cosine, sine):
    low = values[:, : cosine.shape[1]]
    lane = lax.broadcasted_iota(jnp.int32, low.shape, 1)
    half = ROT // 2
    partner = jnp.where(
        lane < half, pltpu.roll(low, low.shape[1] - half, 1), pltpu.roll(low, half, 1)
    )
    return jnp.concatenate([low * cosine + partner * sine, values[:, cosine.shape[1] :]], axis=1)


def attention_kernel(
    order, first, qkv, bias, upstream, cosine, sine, context, context_rel, grads, keys, values,
    score, prob_grad, key_sum, value_sum,
):
    step = pl.program_id(0)
    total = pl.num_programs(0)
    size = HEAD_SIZE
    span = qkv.shape[1]
    last = (((1,), (1,)), ((), ()))
    rows = (((0,), (0,)), ((), ()))
    mine = order[step]
    start = first[step]
    cos_here, sin_here = cosine[mine], sine[mine]
    joined = qkv[0].astype(F32) + bias[...]
    query = (turn(joined[:, :size], cos_here, sin_here) * (size**-0.5)).astype(BF)
    at = pl.ds(pl.multiple_of(step * span, span), span)
    keys[at, :] = turn(joined[:, size : 2 * size], cos_here, sin_here).astype(BF)
    values[at, :] = joined[:, 2 * size :].astype(BF)
    key_sum[at, :] = jnp.zeros((span, size), F32)
    value_sum[at, :] = jnp.zeros((span, size), F32)
    up = upstream[0]

    def one(count):
        blocks = [slice(i * span, (i + 1) * span) for i in range(count)]
        top = jnp.full((span, 1), NEG_FILL, F32)
        for i, block in enumerate(blocks):
            part = lax.dot_general(query, keys[block, :], last, preferred_element_type=F32)
            if i == count - 1:
                row = lax.broadcasted_iota(jnp.int32, part.shape, 0)
                column = lax.broadcasted_iota(jnp.int32, part.shape, 1)
                part = jnp.where(column <= row, part, NEG_FILL)
            else:
                part = part + jnp.where(i >= start, 0.0, NEG_FILL)
            score[:, block] = part
            top = jnp.maximum(top, jnp.max(part, axis=1, keepdims=True))
        norm = jnp.zeros((span, 1), F32)
        for block in blocks:
            part = jnp.exp(score[:, block] - top)
            score[:, block] = part
            norm = norm + jnp.sum(part, axis=1, keepdims=True)
        inverse = 1.0 / norm
        out = jnp.zeros((span, size), F32)
        inner = jnp.zeros((span, 1), F32)
        for block in blocks:
            probs = score[:, block] * inverse
            score[:, block] = probs
            grad = lax.dot_general(up, values[block, :], last, preferred_element_type=F32)
            prob_grad[:, block] = grad
            inner = inner + jnp.sum(probs * grad, axis=1, keepdims=True)
            low = probs.astype(BF)
            out = out + jnp.dot(low, values[block, :], preferred_element_type=F32)
            value_sum[block, :] += lax.dot_general(low, up, rows, preferred_element_type=F32)
        context[0] = out.astype(BF)
        context_rel[0] = out.astype(BF)
        query_grad = jnp.zeros((span, size), F32)
        for block in blocks:
            low = (score[:, block] * (prob_grad[:, block] - inner)).astype(BF)
            query_grad = query_grad + jnp.dot(low, keys[block, :], preferred_element_type=F32)
            key_sum[block, :] += lax.dot_general(low, query, rows, preferred_element_type=F32)
        query_grad = (query_grad * (size**-0.5)).astype(BF).astype(F32)
        grads[mine, :, :size] = turn(query_grad, cos_here, -sin_here).astype(BF)

    steps = keys.shape[0] // span
    for index in range(steps):
        pl.when(step == index)(functools.partial(one, index + 1))

    @pl.when(step == total - 1)
    def finish():
        def each(index, carry):
            place = order[index]
            block = pl.ds(pl.multiple_of(index * span, span), span)
            key_grad = key_sum[block, :].astype(BF).astype(F32)
            grads[place, :, size : 2 * size] = turn(key_grad, cosine[place], -sine[place]).astype(
                BF
            )
            grads[place, :, 2 * size :] = value_sum[block, :].astype(BF)
            return carry

        lax.fori_loop(0, total, each, 0)


def attention(order, first, qkv, bias, upstream, cosine, sine):
    count, span, width = qkv.shape
    size = HEAD_SIZE
    length = count * span
    whole = lambda *shape: pl.BlockSpec(shape, lambda i, o, f: (0,) * len(shape))
    taken = lambda *shape: pl.BlockSpec(
        (1,) + shape, lambda i, o, f: (o[i],) + (0,) * len(shape)
    )
    pairs = count * (count + 1) // 2
    return pl.pallas_call(
        attention_kernel,
        grid_spec=pltpu.PrefetchScalarGridSpec(
            num_scalar_prefetch=2,
            grid=(count,),
            in_specs=[
                taken(span, width),
                whole(1, width),
                taken(span, size),
                whole(count, span, cosine.shape[-1]),
                whole(count, span, cosine.shape[-1]),
            ],
            out_specs=[
                pl.BlockSpec((1, span, size), lambda i, o, f: (i, 0, 0)),
                taken(span, size),
                whole(count, span, width),
            ],
            scratch_shapes=[
                pltpu.VMEM((length, size), BF),
                pltpu.VMEM((length, size), BF),
                pltpu.VMEM((span, length), F32),
                pltpu.VMEM((span, length), F32),
                pltpu.VMEM((length, size), F32),
                pltpu.VMEM((length, size), F32),
            ],
        ),
        out_shape=[
            jax.ShapeDtypeStruct((count, span, size), BF),
            jax.ShapeDtypeStruct((count, span, size), BF),
            jax.ShapeDtypeStruct((count, span, width), BF),
        ],
        compiler_params=ROOM,
        cost_estimate=LIGHT,
        name="attention",
    )(order, first, qkv, bias, upstream, cosine, sine)


def segment_start(lengths, at):
    lengths = lengths.reshape(-1)
    starts = jnp.stack([jnp.sum(lengths[:i]) for i in range(lengths.shape[0])])
    return jnp.max(jnp.where(starts[None, :] <= at[:, None], starts[None, :], 0), axis=1).astype(
        jnp.int32
    )


def rotary_tables(lengths, places, span):
    at = places * span
    offset = (at - segment_start(lengths, at))[:, None] + jnp.arange(span, dtype=jnp.int32)[None, :]
    half = ROT // 2
    frequency = ROT_BASE ** (-(2.0 * jnp.arange(half, dtype=F32)) / ROT)
    angles = offset.astype(F32)[..., None] * frequency
    cosine, sine = jnp.cos(angles), jnp.sin(angles)
    rest = jnp.zeros(offset.shape + (128 - ROT,), F32)
    return (
        jnp.concatenate([cosine, cosine, rest + 1.0], axis=-1),
        jnp.concatenate([-sine, sine, rest], axis=-1),
    )


def body(
    block_in,
    cotangent,
    seg_lengths,
    ln1_gain,
    ln1_bias,
    qkv_weight,
    qkv_bias,
    out_weight,
    out_bias,
    ln2_gain,
    ln2_bias,
    fc1_weight,
    fc1_bias,
    fc2_weight,
    fc2_bias,
):
    rows_here, span, width = block_in.shape
    shard, hidden_units = fc1_weight.shape
    data_count = lax.axis_size("dp")
    head_count = lax.axis_size("head")
    blk_count = lax.axis_size("blk")
    plane = head_count * blk_count
    head_place = lax.axis_index("head")
    blk_place = lax.axis_index("blk")
    place = head_place * blk_count + blk_place
    each = hidden_units // plane
    length = plane * span

    places = [
        (head_place ^ (r % head_count)) * blk_count + (blk_place ^ (r // head_count))
        for r in range(plane)
    ]
    absolute = jnp.arange(plane, dtype=jnp.int32)
    order = (absolute % blk_count ^ blk_place) * head_count + (absolute // blk_count ^ head_place)

    def columns(values, wide):
        return lax.dynamic_slice_in_dim(values, place * wide, wide, 1)

    own_in = block_in.reshape(span, width)
    own_up = cotangent.reshape(span, width)
    att_shard = jnp.concatenate(
        [
            columns(qkv_weight[:, part * width : (part + 1) * width], HEAD_SIZE)
            for part in range(3)
        ]
        + [columns(out_weight, HEAD_SIZE)],
        axis=1,
    )
    att_shard, own_in = tie(att_shard, own_in)
    att_mine = data_gather(att_shard)
    tokens_begun = gather_start(own_in)
    tokens_begun, own_up = tie(tokens_begun, own_up)
    upstream_begun = gather_start(own_up)
    tokens_near, tokens_far = gather_end(*gather_middle(*tokens_begun))
    fc1_shard, tokens_near = tie(columns(fc1_weight, each), tokens_near)
    fc1_mine = data_gather(fc1_shard)
    upstream_begun, tokens_near, tokens_far = tie(upstream_begun, tokens_near, tokens_far)
    upstream_begun = gather_middle(*upstream_begun)
    cosine, sine = rotary_tables(seg_lengths, jnp.stack(places), span)
    normed, attn_in, mlp_in = norms(
        tokens_near, tokens_far, span, ln1_gain, ln1_bias, ln2_gain, ln2_bias
    )
    upstream_begun, attn_in, cosine, sine = tie(upstream_begun, attn_in, cosine, sine)
    upstream_near, upstream_far = gather_end(*upstream_begun)
    upstream_near, att_mine, attn_in = tie(upstream_near, att_mine, attn_in)

    first = segment_start(seg_lengths, absolute * span) // span

    qkv_mine, out_mine = att_mine[:, : 3 * HEAD_SIZE], att_mine[:, 3 * HEAD_SIZE :]
    out_rows = lax.all_to_all(out_mine, ("head", "blk"), split_axis=0, concat_axis=1, tiled=True)
    joined = product(attn_in, qkv_mine, NN, kind=F32)
    upstream_near, upstream_far, joined = tie(upstream_near, upstream_far, joined)
    upstream = jnp.concatenate([upstream_near, upstream_far], axis=0)
    context_grad = product(upstream, out_rows, NT)
    bias_mine = jnp.concatenate(
        [
            lax.dynamic_slice_in_dim(qkv_bias, part * width + place * HEAD_SIZE, HEAD_SIZE, 0)
            for part in range(3)
        ]
    ).astype(F32)
    context_abs, context, qkv_grad = attention(
        order.astype(jnp.int32),
        first,
        joined.reshape(plane, span, 3 * HEAD_SIZE),
        bias_mine[None, :],
        context_grad.reshape(plane, span, HEAD_SIZE),
        cosine,
        sine,
    )
    context = context.reshape(length, HEAD_SIZE)
    qkv_grad = qkv_grad.reshape(length, 3 * HEAD_SIZE)
    out_grad = wide_product(context, upstream)
    out_grad = lax.all_to_all(out_grad, ("head", "blk"), split_axis=1, concat_axis=0, tiled=True)
    qkv_w_grad = product(attn_in, qkv_grad, TN)
    att_grad = jnp.concatenate([qkv_w_grad, out_grad], axis=1)

    fc1_mine, att_grad, context_abs, out_mine, fc2_shard = tie(
        fc1_mine, att_grad, context_abs, out_mine, columns(fc2_weight, each)
    )
    chain = data_count == 4
    if chain:
        move_one = exchange_one(fc2_shard, att_grad)
    else:
        fc2_mine, att_sum = data_gather(fc2_shard), data_scatter(att_grad)
    out_moved = gather_start(out_mine)
    fc1_bias_mine = lax.dynamic_slice_in_dim(fc1_bias, place * each, each, 0).astype(F32)
    active, slope = hidden_units_of(mlp_in, fc1_mine, fc1_bias_mine[None, :])
    if chain:
        move_one, out_moved, fc2_shard, att_grad, active = tie(
            move_one, out_moved, fc2_shard, att_grad, active
        )
        move_two = exchange_two(fc2_shard, att_grad, *move_one)
    out_moved = gather_middle(*out_moved)
    fc2_grad = product(upstream, active, TN)
    if chain:
        move_two, out_moved, att_grad, fc2_grad, context_abs = tie(
            move_two, out_moved, att_grad, fc2_grad, context_abs
        )
        move_three = exchange_three(att_grad, *move_two)
    own_context = lax.all_to_all(
        context_abs.reshape(length, HEAD_SIZE),
        ("head", "blk"),
        split_axis=0,
        concat_axis=1,
        tiled=True,
    )
    if chain:
        move_three, att_grad, own_context, out_moved = tie(
            move_three, att_grad, own_context, out_moved
        )
        move_four = exchange_four(att_grad, *move_three)
    out_pieces = gather_end(*out_moved)
    attn_out = jnp.zeros((span, width), F32)
    for half, pieces in enumerate(out_pieces):
        for index in range(head_count):
            attn_out = lax.dynamic_update_slice(
                attn_out,
                jnp.dot(
                    own_context,
                    pieces[index * width : (index + 1) * width],
                    preferred_element_type=F32,
                ),
                (0, places[half * head_count + index] * HEAD_SIZE),
            )
    attn_out = attn_out + out_bias
    if chain:
        move_four, fc2_grad, attn_out = tie(move_four, fc2_grad, attn_out)
        fc2_mine, att_sum = exchange_end(
            fc2_shard, att_grad, move_one, move_two, move_three, move_four
        )
    fc2_sum = data_scatter(fc2_grad)

    att_moved = gather_start(att_sum)
    mlp_far = product_far(active, fc2_mine)
    mlp_got = other_core(mlp_far)
    hidden_grad, fc1_bias_part = hidden_grad_of(upstream, fc2_mine, slope)
    att_moved, mlp_got, hidden_grad, active = tie(att_moved, mlp_got, hidden_grad, active)
    att_moved = gather_middle(*att_moved)
    mlp_parts = product_near(active, fc2_mine, mlp_got, span)
    att_moved, mlp_parts, hidden_grad = tie(att_moved, mlp_parts, hidden_grad)
    mlp_got = collect_start(*mlp_parts)
    gains = (ln1_gain.astype(F32)[None, :], ln2_gain.astype(F32)[None, :])
    share_far, sums_far = shares(
        False, qkv_grad, qkv_mine, hidden_grad, fc1_mine, gains, normed, span
    )
    mlp_got, share_far, hidden_grad = tie(mlp_got, share_far, hidden_grad)
    mlp_done = collect_middle(mlp_parts, mlp_got)
    share_got = other_core(share_far)
    fc1_low, fc1_high = halves_product(mlp_in, hidden_grad)
    mlp_done, share_got, fc1_low, fc1_high, hidden_grad, fc2_sum = tie(
        mlp_done, share_got, fc1_low, fc1_high, hidden_grad, fc2_sum
    )
    low_sum = data_scatter(fc1_low)
    high_sum = data_scatter(fc1_high)
    fc2_moved = gather_start(fc2_sum)
    *share_parts, sums_near = shares(
        True, qkv_grad, qkv_mine, hidden_grad, fc1_mine, gains, normed, span, share_got
    )
    fc2_moved, share_parts, att_moved = tie(fc2_moved, share_parts, att_moved)
    share_got = collect_start(*share_parts)
    fc2_moved = gather_middle(*fc2_moved)
    place_list = jnp.stack(places).astype(jnp.int32)
    qkv_out, out_out = spread_columns(*gather_end(*att_moved), place_list, (3, 1))
    mlp_out = collect_end(*mlp_done) + fc2_bias
    own_float = own_in.astype(F32)
    block_out = (own_float + attn_out + mlp_out).astype(BF).reshape(block_in.shape)

    moves = sum_moves()
    qkv_bias_part = jnp.sum(qkv_grad.astype(F32), axis=0).reshape(3, 1, HEAD_SIZE)
    here = (jnp.arange(plane) == place).astype(F32)
    norm_sums = sums_far + sums_near
    terms = (
        norm_sums[0],
        norm_sums[1],
        (qkv_bias_part * here[None, :, None]).reshape(-1),
        jnp.sum(own_up.astype(F32), axis=0),
        norm_sums[2],
        norm_sums[3],
        (here[:, None] * fc1_bias_part).reshape(-1),
        jnp.stack([jnp.sum(attn_out * attn_out), jnp.sum(mlp_out * mlp_out)]),
    )
    sizes = [term.shape[0] for term in terms]
    vector = jnp.concatenate(terms + (jnp.zeros((-sum(sizes) % 1024,), F32),)).reshape(-1, 128)
    vector = sum_move(vector, moves[0])

    share_got, fc2_moved, vector, low_sum, qkv_out, out_out = tie(
        share_got, fc2_moved, vector, low_sum, qkv_out, out_out
    )
    share_done = collect_middle(share_parts, share_got)
    low_moved = gather_start(low_sum)
    fc2_moved = gather_end(*fc2_moved)
    vector = sum_move(vector, moves[1])
    share_done, fc2_moved, vector, low_moved, high_sum = tie(
        share_done, fc2_moved, vector, low_moved, high_sum
    )

    share = collect_end(*share_done)
    own_centred = own_float - jnp.mean(own_float, axis=-1, keepdims=True)
    own_scaled = lax.rsqrt(jnp.mean(own_centred * own_centred, axis=-1, keepdims=True) + NORM_EPS)
    own_normed = own_centred * own_scaled
    share = own_scaled * (
        share
        - jnp.mean(share, axis=-1, keepdims=True)
        - own_normed * jnp.mean(share * own_normed, axis=-1, keepdims=True)
    )
    input_grad = (own_up.astype(F32) + share).astype(BF).reshape(block_in.shape)

    low_moved = gather_middle(*low_moved)
    high_moved = gather_start(high_sum)
    vector = sum_move(vector, moves[2])
    [fc2_out] = spread_columns(*fc2_moved, place_list, (1,))
    low_moved, high_moved, vector, fc2_out, input_grad = tie(
        low_moved, high_moved, vector, fc2_out, input_grad
    )
    low_moved = gather_end(*low_moved)
    high_moved = gather_middle(*high_moved)
    vector = sum_move(vector, moves[3])
    low_moved, high_moved, vector = tie(low_moved, high_moved, vector)
    high_moved = gather_end(*high_moved)
    for move in moves[4:]:
        vector = sum_move(vector, move)
    fc1_begun = spread_half(*low_moved, place_list, 0, 0)
    fc1_out = spread_half(*high_moved, place_list, 1, 0, fc1_begun)
    reduced = [
        vector.reshape(-1)[sum(sizes[:i]) : sum(sizes[: i + 1])] for i in range(len(sizes))
    ]
    entries = rows_here * length * data_count * width
    branch_rms = jnp.sqrt(reduced[7] / entries)
    return (
        block_out,
        input_grad,
        reduced[0],
        reduced[1],
        qkv_out,
        reduced[2],
        out_out,
        reduced[3],
        reduced[4],
        reduced[5],
        fc1_out,
        reduced[6],
        fc2_out,
        reduced[3],
        branch_rms[0],
        branch_rms[1],
    )


def solution(mesh):
    rows, tokens, whole = P("dp", None), P("dp", ("head", "blk"), None), P()
    return jax.shard_map(
        body,
        mesh=mesh,
        in_specs=(
            tokens,
            tokens,
            rows,
            whole,
            whole,
            rows,
            whole,
            rows,
            whole,
            whole,
            whole,
            rows,
            whole,
            rows,
            whole,
        ),
        out_specs=(
            tokens,
            tokens,
            whole,
            whole,
            rows,
            whole,
            rows,
            whole,
            whole,
            whole,
            rows,
            whole,
            rows,
            whole,
            whole,
            whole,
        ),
        check_vma=False,
    )
```

```python
import functools

import jax
import jax.numpy as jnp
from jax import lax
from jax.experimental import pallas as pl
from jax.experimental.pallas import tpu as pltpu
from jax.sharding import PartitionSpec as P

HEADS = 8
HEAD_SIZE = 256
ROT = 64
NORM_EPS = 1e-05
NEG_FILL = -1e30
ROT_BASE = 10000.0
BF = jnp.bfloat16
F32 = jnp.float32
NN = (((1,), (0,)), ((), ()))
NT = (((1,), (1,)), ((), ()))
TN = (((0,), (0,)), ((), ()))
LIGHT = pl.CostEstimate(flops=10**9, bytes_accessed=10**6, transcendentals=0)
ROOM = pltpu.CompilerParams(vmem_limit_bytes=48 * 2**20)
MORE_ROOM = pltpu.CompilerParams(vmem_limit_bytes=48 * 2**20)


def across(values, offset):
    count = lax.axis_size("head")
    return lax.ppermute(values, "head", [(i, i ^ offset) for i in range(count)])


def other_core(values):
    return lax.ppermute(values, "blk", [(0, 1), (1, 0)])


def tie(*trees):
    leaves, form = jax.tree.flatten(trees)
    return jax.tree.unflatten(form, lax.optimization_barrier(leaves))


def gather_start(own):
    return own, across(own, 1), across(own, 2)


def gather_middle(own, one, two):
    half = own.shape[0] // 2
    return own, one, two, across(one[:half], 2), across(two[half:], 1)


def gather_end(*pieces):
    near = join(*pieces)
    return near, other_core(near)


def data_gather(own):
    return lax.all_gather(own, "dp", axis=0, tiled=True)


def data_scatter(partial):
    return lax.psum_scatter(partial, "dp", scatter_dimension=0, tiled=True)


def hop_up(values):
    return lax.ppermute(values, "dp", [(0, 1), (1, 2), (2, 3)])


def hop_down(values):
    return lax.ppermute(values, "dp", [(3, 2), (2, 1), (1, 0)])


def part_of(sums, index):
    rows = sums.shape[0] // 4
    return lax.dynamic_slice_in_dim(sums, index * rows, rows, 0)


def exchange_one(own, sums):
    place = lax.axis_index("dp")
    return (
        hop_up(jnp.where(place == 0, part_of(sums, 3), own)),
        hop_down(jnp.where(place == 3, part_of(sums, 0), own)),
    )


def exchange_two(own, sums, up, down):
    place = lax.axis_index("dp")
    up = jnp.where(place == 0, own, jnp.where(place == 1, plus(part_of(sums, 3), up), up))
    down = jnp.where(place == 3, own, jnp.where(place == 2, plus(part_of(sums, 0), down), down))
    return hop_up(up), hop_down(down)


def exchange_three(sums, up, down):
    place = lax.axis_index("dp")
    more_up = plus(part_of(sums, 3), up)
    more_down = plus(part_of(sums, 0), down)
    up = jnp.where(place == 0, part_of(sums, 2), jnp.where(place == 2, more_up, up))
    down = jnp.where(place == 3, part_of(sums, 1), jnp.where(place == 1, more_down, down))
    return hop_up(up), hop_down(down)


def exchange_four(sums, up, down):
    place = lax.axis_index("dp")
    more_up = plus(part_of(sums, 2), up)
    more_down = plus(part_of(sums, 1), down)
    up = jnp.where(place == 0, part_of(sums, 1), jnp.where(place == 1, more_up, up))
    down = jnp.where(place == 3, part_of(sums, 2), jnp.where(place == 2, more_down, down))
    return hop_up(up), hop_down(down)


def exchange_end(own, sums, one, two, three, four):
    place = lax.axis_index("dp")
    rows = own.shape[0]

    def choose(*values):
        out = values[-1]
        for index in range(len(values) - 2, -1, -1):
            if values[index] is not out:
                out = jnp.where(place == index, values[index], out)
        return out

    first = choose(three[1], four[0], four[0], three[0]).astype(F32)
    inner = (place == 1) | (place == 2)
    second = jnp.where(inner, four[1].astype(F32), 0.0)
    total = part_of(sums, place).astype(F32) + first + second
    total, own, one, two, three, four = tie(total.astype(BF), own, one, two, three, four)
    up, down = 0, 1
    whole = jnp.zeros((4 * rows,) + own.shape[1:], own.dtype)
    for step, piece in enumerate(
        (
            own,
            jnp.where(place < 2, one[down], choose(two[down], two[down], two[down], four[up])),
            choose(two[down], three[down], three[up], two[up]),
            jnp.where(place >= 2, one[up], choose(four[down], two[up], two[up], two[up])),
        )
    ):
        whole = lax.dynamic_update_slice_in_dim(whole, piece, (place + step) % 4 * rows, 0)
    return total, whole


def plus(one, two):
    return (one.astype(F32) + two.astype(F32)).astype(BF)


def sum_moves():
    moves = []
    for axis in ("blk", "head", "dp"):
        count = lax.axis_size(axis)
        moves += [
            (axis, [(i, i ^ 2**k) for i in range(count)]) for k in range(count.bit_length() - 1)
        ]
    return moves


def sum_move(vector, move):
    return vector + lax.ppermute(vector, *move)


def whole(array):
    return pl.BlockSpec(array.shape, lambda i: (0,) * array.ndim)


def product(one, two, dims, tile=512, kind=BF):
    def kernel(left, right, out):
        out[...] = lax.dot_general(
            left[...], right[...], dims, preferred_element_type=F32
        ).astype(out.dtype)

    if dims == TN:
        rows, left_spec = one.shape[1], pl.BlockSpec((one.shape[0], tile), lambda i: (0, i))
    else:
        rows, left_spec = one.shape[0], pl.BlockSpec((tile, one.shape[1]), lambda i: (i, 0))
    columns = two.shape[0] if dims == NT else two.shape[1]
    return pl.pallas_call(
        kernel,
        grid=(rows // tile,),
        in_specs=[left_spec, whole(two)],
        out_specs=pl.BlockSpec((tile, columns), lambda i: (i, 0)),
        out_shape=jax.ShapeDtypeStruct((rows, columns), kind),
        compiler_params=ROOM,
        cost_estimate=LIGHT,
        name="product",
    )(one, two)


def wide_product(one, two, tile=512):
    def kernel(left, right, out):
        out[...] = lax.dot_general(
            left[...], right[...], TN, preferred_element_type=F32
        ).astype(BF)

    return pl.pallas_call(
        kernel,
        grid=(two.shape[1] // tile,),
        in_specs=[whole(one), pl.BlockSpec((two.shape[0], tile), lambda i: (0, i))],
        out_specs=pl.BlockSpec((one.shape[1], tile), lambda i: (0, i)),
        out_shape=jax.ShapeDtypeStruct((one.shape[1], two.shape[1]), BF),
        compiler_params=ROOM,
        cost_estimate=LIGHT,
        name="wide",
    )(one, two)


def hidden_kernel(tokens, weight, bias, active, slope):
    hidden = jnp.dot(tokens[...], weight[...], preferred_element_type=F32) + bias[...]
    phi = 0.5 * (1.0 + lax.erf(hidden * (0.5**0.5)))
    active[...] = (hidden * phi).astype(BF)
    density = jnp.exp(-0.5 * hidden * hidden) * ((2.0 * jnp.pi) ** -0.5)
    slope[...] = (phi + hidden * density).astype(BF)


def hidden_units_of(tokens, weight, bias, tile=512):
    rows, width = tokens.shape
    wide = weight.shape[1]
    out = pl.BlockSpec((tile, wide), lambda i: (i, 0))
    return pl.pallas_call(
        hidden_kernel,
        grid=(rows // tile,),
        in_specs=[pl.BlockSpec((tile, width), lambda i: (i, 0)), whole(weight), whole(bias)],
        out_specs=[out, out],
        out_shape=[jax.ShapeDtypeStruct((rows, wide), BF)] * 2,
        compiler_params=MORE_ROOM,
        cost_estimate=LIGHT,
        name="hidden",
    )(tokens, weight, bias)


def hidden_grad_kernel(upstream, weight, slope, grad, total):
    values = jnp.dot(upstream[...], weight[...], preferred_element_type=F32)
    low = (values * slope[...].astype(F32)).astype(BF)
    grad[...] = low

    @pl.when(pl.program_id(0) == 0)
    def clear():
        total[...] = jnp.zeros_like(total)

    total[...] += jnp.sum(low.astype(F32), axis=0, keepdims=True)


def hidden_grad_of(upstream, weight, slope, tile=512):
    rows, width = upstream.shape
    wide = weight.shape[1]
    out = pl.BlockSpec((tile, wide), lambda i: (i, 0))
    return pl.pallas_call(
        hidden_grad_kernel,
        grid=(rows // tile,),
        in_specs=[pl.BlockSpec((tile, width), lambda i: (i, 0)), whole(weight), out],
        out_specs=[out, pl.BlockSpec((1, wide), lambda i: (0, 0))],
        out_shape=[
            jax.ShapeDtypeStruct((rows, wide), BF),
            jax.ShapeDtypeStruct((1, wide), F32),
        ],
        compiler_params=MORE_ROOM,
        cost_estimate=LIGHT,
        name="hidden_grad",
    )(upstream, weight, slope)


def put_split(step, side, block, left_keep, left_send, right_keep, right_send):
    left, right = block[:, :side], block[:, side:]
    for index, out, at in ((0, left_keep, 0), (1, left_send, 0), (2, left_keep, 1), (3, left_send, 1)):

        @pl.when(step == index)
        def write_left(out=out, at=at):
            out[at] = left

    for index, out, at in ((0, right_keep, 0), (1, right_keep, 1), (2, right_send, 0), (3, right_send, 1)):

        @pl.when(step == index)
        def write_right(out=out, at=at):
            out[at] = right


def split_shapes(span, width):
    return [jax.ShapeDtypeStruct((2, span, width // 2), BF)] * 4


def split_specs(span, width):
    return [pl.BlockSpec((2, span, width // 2), lambda i: (0, 0, 0))] * 4


def collect_start(left_keep, left_send, right_keep, right_send):
    return across(left_send, 1), across(right_send, 2)


def collect_middle(parts, got):
    (left_keep, _, right_keep, _), (left, right) = parts, got
    left_last = across(plus(left_keep[1], left[1]), 2)
    right_last = across(plus(right_keep[1], right[1]), 1)
    return (left_keep[0], left[0], left_last), (right_keep[0], right[0], right_last)


def collect_end(*sides):
    return jnp.concatenate(
        [sum(term.astype(F32) for term in terms[1:]) + terms[0].astype(F32) for terms in sides],
        axis=1,
    )


def product_far(one, two, tile=512):
    rows = one.shape[0] // 2

    def kernel(left, right, out):
        out[...] = lax.dot_general(
            left[...], right[...], NT, preferred_element_type=F32
        ).astype(BF)

    return pl.pallas_call(
        kernel,
        grid=(rows // tile,),
        in_specs=[
            pl.BlockSpec((tile, one.shape[1]), lambda i: (i + rows // tile, 0)),
            whole(two),
        ],
        out_specs=pl.BlockSpec((tile, two.shape[0]), lambda i: (i, 0)),
        out_shape=jax.ShapeDtypeStruct((rows, two.shape[0]), BF),
        compiler_params=ROOM,
        cost_estimate=LIGHT,
        name="far",
    )(one, two)


def product_near(one, two, got, span):
    width = two.shape[0]

    def kernel(left, right, more, *outs):
        values = lax.dot_general(left[...], right[...], NT, preferred_element_type=F32)
        block = (values + more[...].astype(F32)).astype(BF)
        put_split(pl.program_id(0), width // 2, block, *outs)

    return pl.pallas_call(
        kernel,
        grid=(one.shape[0] // 2 // span,),
        in_specs=[
            pl.BlockSpec((span, one.shape[1]), lambda i: (i, 0)),
            whole(two),
            pl.BlockSpec((span, width), lambda i: (i, 0)),
        ],
        out_specs=split_specs(span, width),
        out_shape=split_shapes(span, width),
        compiler_params=MORE_ROOM,
        cost_estimate=LIGHT,
        name="near",
    )(one, two, got)


def share_kernel(near, qkv, qkv_weight, hidden, weight, gain_one, gain_two, normed, *rest):
    outs, sums = rest[-5:-1] if near else rest[:1], rest[-1]
    one = lax.dot_general(qkv[...], qkv_weight[...], NT, preferred_element_type=F32)
    two = lax.dot_general(hidden[...], weight[...], NT, preferred_element_type=F32)
    scaled = normed[...].astype(F32)

    @pl.when(pl.program_id(0) == 0)
    def clear():
        sums[...] = jnp.zeros_like(sums)

    for row, values in enumerate((one * scaled, one, two * scaled, two)):
        sums[row : row + 1, :] += jnp.sum(values, axis=0, keepdims=True)
    share = one * gain_one[...] + two * gain_two[...]
    if near:
        block = (share + rest[0][...].astype(F32)).astype(BF)
        put_split(pl.program_id(0), share.shape[1] // 2, block, *outs)
    else:
        outs[0][...] = share.astype(BF)


def shares(near, qkv, qkv_weight, hidden, weight, gains, normed, span, got=None):
    rows, width = normed.shape
    steps = rows // 2 // span
    offset = 0 if near else steps

    def rows_of(array):
        return pl.BlockSpec((span, array.shape[1]), lambda i: (i + offset, 0))

    extra = [got] if near else []
    block = pl.BlockSpec((span, width), lambda i: (i, 0))
    return pl.pallas_call(
        functools.partial(share_kernel, near),
        grid=(steps,),
        in_specs=[
            rows_of(qkv),
            whole(qkv_weight),
            rows_of(hidden),
            whole(weight),
            whole(gains[0]),
            whole(gains[1]),
            rows_of(normed),
        ]
        + [block] * len(extra),
        out_specs=(split_specs(span, width) if near else [block])
        + [pl.BlockSpec((8, width), lambda i: (0, 0))],
        out_shape=(
            split_shapes(span, width) if near else [jax.ShapeDtypeStruct((rows // 2, width), BF)]
        )
        + [jax.ShapeDtypeStruct((8, width), F32)],
        compiler_params=MORE_ROOM,
        cost_estimate=LIGHT,
        name="share_near" if near else "share_far",
    )(qkv, qkv_weight, hidden, weight, *gains, normed, *extra)


def norm_kernel(near, far, gain_one, bias_one, gain_two, bias_two, normed, attn_in, mlp_in):
    half = pl.num_programs(0) // 2

    def write(block):
        values = block[...].astype(F32)
        centred = values - jnp.mean(values, axis=1, keepdims=True)
        spread = jnp.mean(centred * centred, axis=1, keepdims=True)
        scaled = centred * lax.rsqrt(spread + NORM_EPS)
        normed[...] = scaled.astype(BF)
        attn_in[...] = (scaled * gain_one[...] + bias_one[...]).astype(BF)
        mlp_in[...] = (scaled * gain_two[...] + bias_two[...]).astype(BF)

    pl.when(pl.program_id(0) < half)(lambda: write(near))
    pl.when(pl.program_id(0) >= half)(lambda: write(far))


def norms(near, far, span, *vectors):
    rows, width = near.shape
    half = rows // span
    vector = pl.BlockSpec((1, width), lambda i: (0, 0))
    block = pl.BlockSpec((span, width), lambda i: (i, 0))
    return pl.pallas_call(
        norm_kernel,
        grid=(2 * half,),
        in_specs=[
            pl.BlockSpec((span, width), lambda i: (jnp.minimum(i, half - 1), 0)),
            pl.BlockSpec((span, width), lambda i: (jnp.maximum(i - half, 0), 0)),
        ]
        + [vector] * 4,
        out_specs=[block] * 3,
        out_shape=[jax.ShapeDtypeStruct((2 * rows, width), BF)] * 3,
        compiler_params=ROOM,
        cost_estimate=LIGHT,
        name="norms",
    )(near, far, *[v.astype(F32)[None, :] for v in vectors])


def join_kernel(own, one, two, low, high, out):
    half = low.shape[0]
    for index, source in enumerate((own, one, two)):

        @pl.when(pl.program_id(0) == index)
        def copy(source=source):
            out[...] = source[...]

    @pl.when(pl.program_id(0) == 3)
    def last():
        out[:half, :] = low[...]
        out[half:, :] = high[...]


def join(*pieces):
    rows, width = pieces[0].shape
    return pl.pallas_call(
        join_kernel,
        grid=(4,),
        in_specs=[whole(piece) for piece in pieces],
        out_specs=pl.BlockSpec((rows, width), lambda i: (i, 0)),
        out_shape=jax.ShapeDtypeStruct((4 * rows, width), BF),
        compiler_params=ROOM,
        cost_estimate=LIGHT,
        name="join",
    )(*pieces)


def columns_kernel(places, values, near, far, out):
    count = pl.num_programs(0) // 2

    def write(source):
        out[...] = jnp.dot(values[...], source[...], preferred_element_type=F32)

    pl.when(pl.program_id(0) < count)(lambda: write(near))
    pl.when(pl.program_id(0) >= count)(lambda: write(far))


def columns_product(values, near, far, places):
    count = lax.axis_size("head")
    rows, depth = values.shape
    width = near.shape[1]
    return pl.pallas_call(
        columns_kernel,
        grid_spec=pltpu.PrefetchScalarGridSpec(
            num_scalar_prefetch=1,
            grid=(2 * count,),
            in_specs=[
                pl.BlockSpec((rows, depth), lambda r, p: (0, 0)),
                pl.BlockSpec((depth, width), lambda r, p: (jnp.minimum(r, count - 1), 0)),
                pl.BlockSpec((depth, width), lambda r, p: (jnp.maximum(r - count, 0), 0)),
            ],
            out_specs=pl.BlockSpec((rows, width), lambda r, p: (0, p[r])),
        ),
        out_shape=jax.ShapeDtypeStruct((rows, 2 * count * width), F32),
        compiler_params=ROOM,
        cost_estimate=LIGHT,
        name="columns",
    )(places, values, near, far)


def spread_kernel(parts, places, near, far, *outs):
    count = near.shape[0]
    each = near.shape[2] // sum(parts)
    for relative in range(2 * count):
        source = near if relative < count else far
        at = 0
        for out, part in zip(outs, parts):
            for index in range(part):
                where = (index * 2 * count + places[relative]) * each
                out[:, pl.ds(pl.multiple_of(where, each), each)] = source[
                    relative % count, :, at * each : (at + 1) * each
                ].astype(F32)
                at += 1


def spread_columns(near, far, places, parts):
    count = lax.axis_size("head")
    rows = near.shape[0] // count
    width = near.shape[1]
    step = min(rows, 64)
    each = width // sum(parts)
    taken = pl.BlockSpec((count, step, width), lambda i, p: (0, i, 0))
    wide = [2 * count * each * part for part in parts]
    return pl.pallas_call(
        functools.partial(spread_kernel, parts),
        grid_spec=pltpu.PrefetchScalarGridSpec(
            num_scalar_prefetch=1,
            grid=(rows // step,),
            in_specs=[taken, taken],
            out_specs=[pl.BlockSpec((step, w), lambda i, p: (i, 0)) for w in wide],
        ),
        out_shape=[jax.ShapeDtypeStruct((rows, w), F32) for w in wide],
        compiler_params=ROOM,
        cost_estimate=LIGHT,
        name="spread",
    )(places, near.reshape(count, rows, width), far.reshape(count, rows, width))


def place_kernel(places, blocks, *rest):
    rest[-1][...] = blocks[...].astype(F32)


def place_blocks(blocks, places, begun=None):
    count = lax.axis_size("head")
    rows, width = blocks.shape[0] // count, blocks.shape[1]
    extra = () if begun is None else (begun,)
    return pl.pallas_call(
        place_kernel,
        grid_spec=pltpu.PrefetchScalarGridSpec(
            num_scalar_prefetch=1,
            grid=(count,),
            in_specs=[pl.BlockSpec((rows, width), lambda r, p: (r, 0))]
            + [pl.BlockSpec(memory_space=pl.ANY) for _ in extra],
            out_specs=pl.BlockSpec((rows, width), lambda r, p: (0, p[r])),
        ),
        out_shape=jax.ShapeDtypeStruct((rows, 2 * count * width), F32),
        input_output_aliases={2: 0} if extra else {},
        compiler_params=ROOM,
        cost_estimate=LIGHT,
        name="place",
    )(places, blocks, *extra)


def turn(values, cosine, sine):
    low = values[:, : cosine.shape[1]]
    lane = lax.broadcasted_iota(jnp.int32, low.shape, 1)
    half = ROT // 2
    partner = jnp.where(
        lane < half, pltpu.roll(low, low.shape[1] - half, 1), pltpu.roll(low, half, 1)
    )
    return jnp.concatenate([low * cosine + partner * sine, values[:, cosine.shape[1] :]], axis=1)


def attention_kernel(
    order, first, qkv, bias, upstream, cosine, sine, context, context_rel, grads, keys, values,
    score, prob_grad, key_sum, value_sum,
):
    step = pl.program_id(0)
    total = pl.num_programs(0)
    size = HEAD_SIZE
    span = qkv.shape[1]
    last = (((1,), (1,)), ((), ()))
    rows = (((0,), (0,)), ((), ()))
    mine = order[step]
    start = first[step]
    cos_here, sin_here = cosine[mine], sine[mine]
    joined = qkv[0].astype(F32) + bias[...]
    query = (turn(joined[:, :size], cos_here, sin_here) * (size**-0.5)).astype(BF)
    at = pl.ds(pl.multiple_of(step * span, span), span)
    keys[at, :] = turn(joined[:, size : 2 * size], cos_here, sin_here).astype(BF)
    values[at, :] = joined[:, 2 * size :].astype(BF)
    key_sum[at, :] = jnp.zeros((span, size), F32)
    value_sum[at, :] = jnp.zeros((span, size), F32)
    up = upstream[0]

    def one(count):
        blocks = [slice(i * span, (i + 1) * span) for i in range(count)]
        top = jnp.full((span, 1), NEG_FILL, F32)
        for i, block in enumerate(blocks):
            part = lax.dot_general(query, keys[block, :], last, preferred_element_type=F32)
            if i == count - 1:
                row = lax.broadcasted_iota(jnp.int32, part.shape, 0)
                column = lax.broadcasted_iota(jnp.int32, part.shape, 1)
                part = jnp.where(column <= row, part, NEG_FILL)
            else:
                part = part + jnp.where(i >= start, 0.0, NEG_FILL)
            score[:, block] = part
            top = jnp.maximum(top, jnp.max(part, axis=1, keepdims=True))
        norm = jnp.zeros((span, 1), F32)
        for block in blocks:
            part = jnp.exp(score[:, block] - top)
            score[:, block] = part
            norm = norm + jnp.sum(part, axis=1, keepdims=True)
        inverse = 1.0 / norm
        out = jnp.zeros((span, size), F32)
        inner = jnp.zeros((span, 1), F32)
        for block in blocks:
            probs = score[:, block] * inverse
            score[:, block] = probs
            grad = lax.dot_general(up, values[block, :], last, preferred_element_type=F32)
            prob_grad[:, block] = grad
            inner = inner + jnp.sum(probs * grad, axis=1, keepdims=True)
            low = probs.astype(BF)
            out = out + jnp.dot(low, values[block, :], preferred_element_type=F32)
            value_sum[block, :] += lax.dot_general(low, up, rows, preferred_element_type=F32)
        context[0] = out.astype(BF)
        context_rel[0] = out.astype(BF)
        query_grad = jnp.zeros((span, size), F32)
        for block in blocks:
            low = (score[:, block] * (prob_grad[:, block] - inner)).astype(BF)
            query_grad = query_grad + jnp.dot(low, keys[block, :], preferred_element_type=F32)
            key_sum[block, :] += lax.dot_general(low, query, rows, preferred_element_type=F32)
        query_grad = (query_grad * (size**-0.5)).astype(BF).astype(F32)
        grads[mine, :, :size] = turn(query_grad, cos_here, -sin_here).astype(BF)

    steps = keys.shape[0] // span
    for index in range(steps):
        pl.when(step == index)(functools.partial(one, index + 1))

    @pl.when(step == total - 1)
    def finish():
        def each(index, carry):
            place = order[index]
            block = pl.ds(pl.multiple_of(index * span, span), span)
            key_grad = key_sum[block, :].astype(BF).astype(F32)
            grads[place, :, size : 2 * size] = turn(key_grad, cosine[place], -sine[place]).astype(
                BF
            )
            grads[place, :, 2 * size :] = value_sum[block, :].astype(BF)
            return carry

        lax.fori_loop(0, total, each, 0)


def attention(order, first, qkv, bias, upstream, cosine, sine):
    count, span, width = qkv.shape
    size = HEAD_SIZE
    length = count * span
    whole = lambda *shape: pl.BlockSpec(shape, lambda i, o, f: (0,) * len(shape))
    taken = lambda *shape: pl.BlockSpec(
        (1,) + shape, lambda i, o, f: (o[i],) + (0,) * len(shape)
    )
    pairs = count * (count + 1) // 2
    return pl.pallas_call(
        attention_kernel,
        grid_spec=pltpu.PrefetchScalarGridSpec(
            num_scalar_prefetch=2,
            grid=(count,),
            in_specs=[
                taken(span, width),
                whole(1, width),
                taken(span, size),
                whole(count, span, cosine.shape[-1]),
                whole(count, span, cosine.shape[-1]),
            ],
            out_specs=[
                pl.BlockSpec((1, span, size), lambda i, o, f: (i, 0, 0)),
                taken(span, size),
                whole(count, span, width),
            ],
            scratch_shapes=[
                pltpu.VMEM((length, size), BF),
                pltpu.VMEM((length, size), BF),
                pltpu.VMEM((span, length), F32),
                pltpu.VMEM((span, length), F32),
                pltpu.VMEM((length, size), F32),
                pltpu.VMEM((length, size), F32),
            ],
        ),
        out_shape=[
            jax.ShapeDtypeStruct((count, span, size), BF),
            jax.ShapeDtypeStruct((count, span, size), BF),
            jax.ShapeDtypeStruct((count, span, width), BF),
        ],
        compiler_params=ROOM,
        cost_estimate=LIGHT,
        name="attention",
    )(order, first, qkv, bias, upstream, cosine, sine)


def segment_start(lengths, at):
    lengths = lengths.reshape(-1)
    starts = jnp.stack([jnp.sum(lengths[:i]) for i in range(lengths.shape[0])])
    return jnp.max(jnp.where(starts[None, :] <= at[:, None], starts[None, :], 0), axis=1).astype(
        jnp.int32
    )


def rotary_tables(lengths, places, span):
    at = places * span
    offset = (at - segment_start(lengths, at))[:, None] + jnp.arange(span, dtype=jnp.int32)[None, :]
    half = ROT // 2
    frequency = ROT_BASE ** (-(2.0 * jnp.arange(half, dtype=F32)) / ROT)
    angles = offset.astype(F32)[..., None] * frequency
    cosine, sine = jnp.cos(angles), jnp.sin(angles)
    rest = jnp.zeros(offset.shape + (128 - ROT,), F32)
    return (
        jnp.concatenate([cosine, cosine, rest + 1.0], axis=-1),
        jnp.concatenate([-sine, sine, rest], axis=-1),
    )


def body(
    block_in,
    cotangent,
    seg_lengths,
    ln1_gain,
    ln1_bias,
    qkv_weight,
    qkv_bias,
    out_weight,
    out_bias,
    ln2_gain,
    ln2_bias,
    fc1_weight,
    fc1_bias,
    fc2_weight,
    fc2_bias,
):
    rows_here, span, width = block_in.shape
    shard, hidden_units = fc1_weight.shape
    data_count = lax.axis_size("dp")
    head_count = lax.axis_size("head")
    blk_count = lax.axis_size("blk")
    plane = head_count * blk_count
    head_place = lax.axis_index("head")
    blk_place = lax.axis_index("blk")
    place = head_place * blk_count + blk_place
    each = hidden_units // plane
    length = plane * span

    places = [
        (head_place ^ (r % head_count)) * blk_count + (blk_place ^ (r // head_count))
        for r in range(plane)
    ]
    place_list = jnp.stack(places).astype(jnp.int32)
    absolute = jnp.arange(plane, dtype=jnp.int32)
    order = (absolute % blk_count ^ blk_place) * head_count + (absolute // blk_count ^ head_place)

    def columns(values, wide):
        return lax.dynamic_slice_in_dim(values, place * wide, wide, 1)

    own_in = block_in.reshape(span, width)
    own_up = cotangent.reshape(span, width)
    out_shard = columns(out_weight, HEAD_SIZE)
    qkv_shard = jnp.concatenate(
        [
            columns(qkv_weight[:, part * width : (part + 1) * width], HEAD_SIZE)
            for part in range(3)
        ],
        axis=1,
    )
    out_shard, own_in = tie(out_shard, own_in)
    out_mine = data_gather(out_shard)
    tokens_begun = gather_start(own_in)
    tokens_begun, own_up, qkv_shard = tie(tokens_begun, own_up, qkv_shard)
    qkv_mine = data_gather(qkv_shard)
    upstream_begun = gather_start(own_up)
    tokens_near, tokens_far = gather_end(*gather_middle(*tokens_begun))
    fc1_shard, tokens_near = tie(columns(fc1_weight, each), tokens_near)
    fc1_mine = data_gather(fc1_shard)
    cosine, sine = rotary_tables(seg_lengths, jnp.stack(places), span)
    normed, attn_in, mlp_in = norms(
        tokens_near, tokens_far, span, ln1_gain, ln1_bias, ln2_gain, ln2_bias
    )
    upstream_begun, attn_in, cosine, sine, out_mine = tie(
        upstream_begun, attn_in, cosine, sine, out_mine
    )
    out_rows = lax.all_to_all(out_mine, ("head", "blk"), split_axis=0, concat_axis=1, tiled=True)
    upstream_near, upstream_far = gather_end(*gather_middle(*upstream_begun))
    upstream_near, qkv_mine, attn_in = tie(upstream_near, qkv_mine, attn_in)

    first = segment_start(seg_lengths, absolute * span) // span

    joined = product(attn_in, qkv_mine, NN, kind=F32)
    upstream_near, upstream_far, joined, out_rows = tie(
        upstream_near, upstream_far, joined, out_rows
    )
    upstream = jnp.concatenate([upstream_near, upstream_far], axis=0)
    context_grad = product(upstream, out_rows, NT)
    bias_mine = jnp.concatenate(
        [
            lax.dynamic_slice_in_dim(qkv_bias, part * width + place * HEAD_SIZE, HEAD_SIZE, 0)
            for part in range(3)
        ]
    ).astype(F32)
    context_abs, context, qkv_grad = attention(
        order.astype(jnp.int32),
        first,
        joined.reshape(plane, span, 3 * HEAD_SIZE),
        bias_mine[None, :],
        context_grad.reshape(plane, span, HEAD_SIZE),
        cosine,
        sine,
    )
    context = context.reshape(length, HEAD_SIZE)
    qkv_grad = qkv_grad.reshape(length, 3 * HEAD_SIZE)
    out_grad = wide_product(context, upstream)
    out_grad = lax.all_to_all(out_grad, ("head", "blk"), split_axis=1, concat_axis=0, tiled=True)
    qkv_w_grad = product(attn_in, qkv_grad, TN)
    att_grad = jnp.concatenate([qkv_w_grad, out_grad], axis=1)

    fc1_mine, att_grad, context_abs, out_mine, fc2_shard = tie(
        fc1_mine, att_grad, context_abs, out_mine, columns(fc2_weight, each)
    )
    chain = data_count == 4
    if chain:
        move_one = exchange_one(fc2_shard, att_grad)
    else:
        fc2_mine, att_sum = data_gather(fc2_shard), data_scatter(att_grad)
    out_moved = gather_start(out_mine)
    fc1_bias_mine = lax.dynamic_slice_in_dim(fc1_bias, place * each, each, 0).astype(F32)
    active, slope = hidden_units_of(mlp_in, fc1_mine, fc1_bias_mine[None, :])
    if chain:
        move_one, out_moved, fc2_shard, att_grad, active = tie(
            move_one, out_moved, fc2_shard, att_grad, active
        )
        move_two = exchange_two(fc2_shard, att_grad, *move_one)
    out_moved = gather_middle(*out_moved)
    fc2_grad = product(upstream, active, TN)
    if chain:
        move_two, out_moved, att_grad, fc2_grad, context_abs = tie(
            move_two, out_moved, att_grad, fc2_grad, context_abs
        )
        move_three = exchange_three(att_grad, *move_two)
    own_context = lax.all_to_all(
        context_abs.reshape(length, HEAD_SIZE),
        ("head", "blk"),
        split_axis=0,
        concat_axis=1,
        tiled=True,
    )
    if chain:
        move_three, att_grad, own_context, out_moved = tie(
            move_three, att_grad, own_context, out_moved
        )
        move_four = exchange_four(att_grad, *move_three)
    if chain:
        move_four, fc2_grad = tie(move_four, fc2_grad)
        att_sum, fc2_mine = exchange_end(
            fc2_shard, att_grad, move_one, move_two, move_three, move_four
        )
    fc2_sum = data_scatter(fc2_grad)

    att_moved = gather_start(att_sum)
    mlp_far = product_far(active, fc2_mine)
    mlp_got = other_core(mlp_far)
    hidden_grad, fc1_bias_part = hidden_grad_of(upstream, fc2_mine, slope)
    att_moved, mlp_got, hidden_grad, active = tie(att_moved, mlp_got, hidden_grad, active)
    att_moved = gather_middle(*att_moved)
    mlp_parts = product_near(active, fc2_mine, mlp_got, span)
    att_moved, mlp_parts, hidden_grad = tie(att_moved, mlp_parts, hidden_grad)
    mlp_got = collect_start(*mlp_parts)
    fc1_grad = product(mlp_in, hidden_grad, TN)
    att_near, out_near = join(*att_moved), join(*out_moved)
    mlp_got, fc1_grad, hidden_grad, fc2_sum, att_near, out_near = tie(
        mlp_got, fc1_grad, hidden_grad, fc2_sum, att_near, out_near
    )
    fc1_sum = data_scatter(fc1_grad)
    mlp_done = collect_middle(mlp_parts, mlp_got)
    att_far, out_far = other_core(att_near), other_core(out_near)
    gains = (ln1_gain.astype(F32)[None, :], ln2_gain.astype(F32)[None, :])
    share_far, sums_far = shares(
        False, qkv_grad, qkv_mine, hidden_grad, fc1_mine, gains, normed, span
    )
    mlp_done, share_far, att_far, out_far, fc2_sum = tie(
        mlp_done, share_far, att_far, out_far, fc2_sum
    )
    share_got = other_core(share_far)
    fc2_moved = gather_start(fc2_sum)
    *share_parts, sums_near = shares(
        True, qkv_grad, qkv_mine, hidden_grad, fc1_mine, gains, normed, span, share_got
    )
    fc2_moved, share_parts, att_far, out_far = tie(fc2_moved, share_parts, att_far, out_far)
    share_got = collect_start(*share_parts)
    fc2_moved = gather_middle(*fc2_moved)
    attn_out = columns_product(own_context, out_near, out_far, place_list) + out_bias
    qkv_out, out_out = spread_columns(att_near, att_far, place_list, (3, 1))
    mlp_out = collect_end(*mlp_done) + fc2_bias
    own_float = own_in.astype(F32)
    block_out = (own_float + attn_out + mlp_out).astype(BF).reshape(block_in.shape)

    moves = sum_moves()
    qkv_bias_part = jnp.sum(qkv_grad.astype(F32), axis=0).reshape(3, 1, HEAD_SIZE)
    here = (jnp.arange(plane) == place).astype(F32)
    norm_sums = sums_far + sums_near
    terms = (
        norm_sums[0],
        norm_sums[1],
        (qkv_bias_part * here[None, :, None]).reshape(-1),
        jnp.sum(own_up.astype(F32), axis=0),
        norm_sums[2],
        norm_sums[3],
        (here[:, None] * fc1_bias_part).reshape(-1),
        jnp.stack([jnp.sum(attn_out * attn_out), jnp.sum(mlp_out * mlp_out)]),
    )
    sizes = [term.shape[0] for term in terms]
    vector = jnp.concatenate(terms + (jnp.zeros((-sum(sizes) % 1024,), F32),)).reshape(-1, 128)
    share_got, fc2_moved, vector, block_out, qkv_out, out_out, fc1_sum = tie(
        share_got, fc2_moved, vector, block_out, qkv_out, out_out, fc1_sum
    )
    share_done = collect_middle(share_parts, share_got)
    fc1_moved = gather_start(fc1_sum)
    vector = sum_move(vector, moves[0])
    share_done, fc1_moved, vector, fc2_moved = tie(share_done, fc1_moved, vector, fc2_moved)
    fc1_moved = gather_middle(*fc1_moved)
    fc2_near, fc2_far = gather_end(*fc2_moved)
    vector = sum_move(sum_move(vector, moves[1]), moves[2])

    share = collect_end(*share_done)
    own_centred = own_float - jnp.mean(own_float, axis=-1, keepdims=True)
    own_scaled = lax.rsqrt(jnp.mean(own_centred * own_centred, axis=-1, keepdims=True) + NORM_EPS)
    own_normed = own_centred * own_scaled
    share = own_scaled * (
        share
        - jnp.mean(share, axis=-1, keepdims=True)
        - own_normed * jnp.mean(share * own_normed, axis=-1, keepdims=True)
    )
    input_grad = (own_up.astype(F32) + share).astype(BF).reshape(block_in.shape)

    fc1_moved, vector, fc2_near, fc2_far, input_grad = tie(
        fc1_moved, vector, fc2_near, fc2_far, input_grad
    )
    fc1_near, fc1_far = gather_end(*fc1_moved)
    fc2_out = place_blocks(fc2_near, place_list[:head_count])
    fc2_out = place_blocks(fc2_far, place_list[head_count:], fc2_out)
    fc1_out = place_blocks(fc1_near, place_list[:head_count])
    for move in moves[3:]:
        vector = sum_move(vector, move)
    fc1_far, fc1_out, fc2_out, vector = tie(fc1_far, fc1_out, fc2_out, vector)
    fc1_out = place_blocks(fc1_far, place_list[head_count:], fc1_out)
    reduced = [
        vector.reshape(-1)[sum(sizes[:i]) : sum(sizes[: i + 1])] for i in range(len(sizes))
    ]
    entries = rows_here * length * data_count * width
    branch_rms = jnp.sqrt(reduced[7] / entries)
    return (
        block_out,
        input_grad,
        reduced[0],
        reduced[1],
        qkv_out,
        reduced[2],
        out_out,
        reduced[3],
        reduced[4],
        reduced[5],
        fc1_out,
        reduced[6],
        fc2_out,
        reduced[3],
        branch_rms[0],
        branch_rms[1],
    )


def solution(mesh):
    rows, tokens, whole = P("dp", None), P("dp", ("head", "blk"), None), P()
    return jax.shard_map(
        body,
        mesh=mesh,
        in_specs=(
            tokens,
            tokens,
            rows,
            whole,
            whole,
            rows,
            whole,
            rows,
            whole,
            whole,
            whole,
            rows,
            whole,
            rows,
            whole,
        ),
        out_specs=(
            tokens,
            tokens,
            whole,
            whole,
            rows,
            whole,
            rows,
            whole,
            whole,
            whole,
            rows,
            whole,
            rows,
            whole,
            whole,
            whole,
        ),
        check_vma=False,
    )
```

```python
import functools

import jax
import jax.numpy as jnp
from jax import lax
from jax.experimental import pallas as pl
from jax.experimental.pallas import tpu as pltpu
from jax.sharding import PartitionSpec as P

HEADS = 8
HEAD_SIZE = 256
ROT = 64
NORM_EPS = 1e-05
NEG_FILL = -1e30
ROT_BASE = 10000.0
BF = jnp.bfloat16
F32 = jnp.float32
NN = (((1,), (0,)), ((), ()))
NT = (((1,), (1,)), ((), ()))
TN = (((0,), (0,)), ((), ()))
LIGHT = pl.CostEstimate(flops=10**9, bytes_accessed=10**6, transcendentals=0)
ROOM = pltpu.CompilerParams(vmem_limit_bytes=48 * 2**20)
MORE_ROOM = pltpu.CompilerParams(vmem_limit_bytes=48 * 2**20)


def across(values, offset):
    count = lax.axis_size("head")
    return lax.ppermute(values, "head", [(i, i ^ offset) for i in range(count)])


def other_core(values):
    return lax.ppermute(values, "blk", [(0, 1), (1, 0)])


def tie(*trees):
    leaves, form = jax.tree.flatten(trees)
    return jax.tree.unflatten(form, lax.optimization_barrier(leaves))


def gather_start(own):
    return own, across(own, 1), across(own, 2)


def gather_middle(own, one, two):
    half = own.shape[0] // 2
    return own, one, two, across(one[:half], 2), across(two[half:], 1)


def gather_end(*pieces):
    near = join(*pieces)
    return near, other_core(near)


def data_gather(own):
    return lax.all_gather(own, "dp", axis=0, tiled=True)


def data_scatter(partial):
    return lax.psum_scatter(partial, "dp", scatter_dimension=0, tiled=True)


def hop_up(values):
    return lax.ppermute(values, "dp", [(0, 1), (1, 2), (2, 3)])


def hop_down(values):
    return lax.ppermute(values, "dp", [(3, 2), (2, 1), (1, 0)])


def part_of(sums, index):
    rows = sums.shape[0] // 4
    return lax.dynamic_slice_in_dim(sums, index * rows, rows, 0)


def exchange_one(own, sums):
    place = lax.axis_index("dp")
    return (
        hop_up(jnp.where(place == 0, part_of(sums, 3), own)),
        hop_down(jnp.where(place == 3, part_of(sums, 0), own)),
    )


def exchange_two(own, sums, up, down):
    place = lax.axis_index("dp")
    up = jnp.where(place == 0, own, jnp.where(place == 1, plus(part_of(sums, 3), up), up))
    down = jnp.where(place == 3, own, jnp.where(place == 2, plus(part_of(sums, 0), down), down))
    return hop_up(up), hop_down(down)


def exchange_three(sums, up, down):
    place = lax.axis_index("dp")
    more_up = plus(part_of(sums, 3), up)
    more_down = plus(part_of(sums, 0), down)
    up = jnp.where(place == 0, part_of(sums, 2), jnp.where(place == 2, more_up, up))
    down = jnp.where(place == 3, part_of(sums, 1), jnp.where(place == 1, more_down, down))
    return hop_up(up), hop_down(down)


def exchange_four(sums, up, down):
    place = lax.axis_index("dp")
    more_up = plus(part_of(sums, 2), up)
    more_down = plus(part_of(sums, 1), down)
    up = jnp.where(place == 0, part_of(sums, 1), jnp.where(place == 1, more_up, up))
    down = jnp.where(place == 3, part_of(sums, 2), jnp.where(place == 2, more_down, down))
    return hop_up(up), hop_down(down)


def exchange_end(own, sums, one, two, three, four):
    place = lax.axis_index("dp")
    rows = own.shape[0]

    def choose(*values):
        out = values[-1]
        for index in range(len(values) - 2, -1, -1):
            if values[index] is not out:
                out = jnp.where(place == index, values[index], out)
        return out

    first = choose(three[1], four[0], four[0], three[0]).astype(F32)
    inner = (place == 1) | (place == 2)
    second = jnp.where(inner, four[1].astype(F32), 0.0)
    total = part_of(sums, place).astype(F32) + first + second
    total, own, one, two, three, four = tie(total.astype(BF), own, one, two, three, four)
    up, down = 0, 1
    whole = jnp.zeros((4 * rows,) + own.shape[1:], own.dtype)
    for step, piece in enumerate(
        (
            own,
            jnp.where(place < 2, one[down], choose(two[down], two[down], two[down], four[up])),
            choose(two[down], three[down], three[up], two[up]),
            jnp.where(place >= 2, one[up], choose(four[down], two[up], two[up], two[up])),
        )
    ):
        whole = lax.dynamic_update_slice_in_dim(whole, piece, (place + step) % 4 * rows, 0)
    return total, whole


def plus(one, two):
    return (one.astype(F32) + two.astype(F32)).astype(BF)


def sum_moves():
    moves = []
    for axis in ("blk", "head", "dp"):
        count = lax.axis_size(axis)
        moves += [
            (axis, [(i, i ^ 2**k) for i in range(count)]) for k in range(count.bit_length() - 1)
        ]
    return moves


def sum_move(vector, move):
    return vector + lax.ppermute(vector, *move)


def whole(array):
    return pl.BlockSpec(array.shape, lambda i: (0,) * array.ndim)


def product(one, two, dims, tile=512, kind=BF):
    def kernel(left, right, out):
        out[...] = lax.dot_general(
            left[...], right[...], dims, preferred_element_type=F32
        ).astype(out.dtype)

    if dims == TN:
        rows, left_spec = one.shape[1], pl.BlockSpec((one.shape[0], tile), lambda i: (0, i))
    else:
        rows, left_spec = one.shape[0], pl.BlockSpec((tile, one.shape[1]), lambda i: (i, 0))
    columns = two.shape[0] if dims == NT else two.shape[1]
    return pl.pallas_call(
        kernel,
        grid=(rows // tile,),
        in_specs=[left_spec, whole(two)],
        out_specs=pl.BlockSpec((tile, columns), lambda i: (i, 0)),
        out_shape=jax.ShapeDtypeStruct((rows, columns), kind),
        compiler_params=ROOM,
        cost_estimate=LIGHT,
        name="product",
    )(one, two)


def wide_product(one, two, tile=512):
    def kernel(left, right, out):
        out[...] = lax.dot_general(
            left[...], right[...], TN, preferred_element_type=F32
        ).astype(BF)

    return pl.pallas_call(
        kernel,
        grid=(two.shape[1] // tile,),
        in_specs=[whole(one), pl.BlockSpec((two.shape[0], tile), lambda i: (0, i))],
        out_specs=pl.BlockSpec((one.shape[1], tile), lambda i: (0, i)),
        out_shape=jax.ShapeDtypeStruct((one.shape[1], two.shape[1]), BF),
        compiler_params=ROOM,
        cost_estimate=LIGHT,
        name="wide",
    )(one, two)


def hidden_kernel(tokens, weight, bias, active, slope):
    hidden = jnp.dot(tokens[...], weight[...], preferred_element_type=F32) + bias[...]
    phi = 0.5 * (1.0 + lax.erf(hidden * (0.5**0.5)))
    active[...] = (hidden * phi).astype(BF)
    density = jnp.exp(-0.5 * hidden * hidden) * ((2.0 * jnp.pi) ** -0.5)
    slope[...] = (phi + hidden * density).astype(BF)


def hidden_units_of(tokens, weight, bias, tile=512):
    rows, width = tokens.shape
    wide = weight.shape[1]
    out = pl.BlockSpec((tile, wide), lambda i: (i, 0))
    return pl.pallas_call(
        hidden_kernel,
        grid=(rows // tile,),
        in_specs=[pl.BlockSpec((tile, width), lambda i: (i, 0)), whole(weight), whole(bias)],
        out_specs=[out, out],
        out_shape=[jax.ShapeDtypeStruct((rows, wide), BF)] * 2,
        compiler_params=MORE_ROOM,
        cost_estimate=LIGHT,
        name="hidden",
    )(tokens, weight, bias)


def hidden_grad_kernel(upstream, weight, slope, grad, total):
    values = jnp.dot(upstream[...], weight[...], preferred_element_type=F32)
    low = (values * slope[...].astype(F32)).astype(BF)
    grad[...] = low

    @pl.when(pl.program_id(0) == 0)
    def clear():
        total[...] = jnp.zeros_like(total)

    total[...] += jnp.sum(low.astype(F32), axis=0, keepdims=True)


def hidden_grad_of(upstream, weight, slope, tile=512):
    rows, width = upstream.shape
    wide = weight.shape[1]
    out = pl.BlockSpec((tile, wide), lambda i: (i, 0))
    return pl.pallas_call(
        hidden_grad_kernel,
        grid=(rows // tile,),
        in_specs=[pl.BlockSpec((tile, width), lambda i: (i, 0)), whole(weight), out],
        out_specs=[out, pl.BlockSpec((1, wide), lambda i: (0, 0))],
        out_shape=[
            jax.ShapeDtypeStruct((rows, wide), BF),
            jax.ShapeDtypeStruct((1, wide), F32),
        ],
        compiler_params=MORE_ROOM,
        cost_estimate=LIGHT,
        name="hidden_grad",
    )(upstream, weight, slope)


def put_split(step, side, block, left_keep, left_send, right_keep, right_send):
    left, right = block[:, :side], block[:, side:]
    for index, out, at in ((0, left_keep, 0), (1, left_send, 0), (2, left_keep, 1), (3, left_send, 1)):

        @pl.when(step == index)
        def write_left(out=out, at=at):
            out[at] = left

    for index, out, at in ((0, right_keep, 0), (1, right_keep, 1), (2, right_send, 0), (3, right_send, 1)):

        @pl.when(step == index)
        def write_right(out=out, at=at):
            out[at] = right


def split_shapes(span, width):
    return [jax.ShapeDtypeStruct((2, span, width // 2), BF)] * 4


def split_specs(span, width):
    return [pl.BlockSpec((2, span, width // 2), lambda i: (0, 0, 0))] * 4


def collect_start(left_keep, left_send, right_keep, right_send):
    return across(left_send, 1), across(right_send, 2)


def collect_middle(parts, got):
    (left_keep, _, right_keep, _), (left, right) = parts, got
    left_last = across(plus(left_keep[1], left[1]), 2)
    right_last = across(plus(right_keep[1], right[1]), 1)
    return (left_keep[0], left[0], left_last), (right_keep[0], right[0], right_last)


def collect_end(*sides):
    return jnp.concatenate(
        [sum(term.astype(F32) for term in terms[1:]) + terms[0].astype(F32) for terms in sides],
        axis=1,
    )


def product_far(one, two, tile=512):
    rows = one.shape[0] // 2

    def kernel(left, right, out):
        out[...] = lax.dot_general(
            left[...], right[...], NT, preferred_element_type=F32
        ).astype(BF)

    return pl.pallas_call(
        kernel,
        grid=(rows // tile,),
        in_specs=[
            pl.BlockSpec((tile, one.shape[1]), lambda i: (i + rows // tile, 0)),
            whole(two),
        ],
        out_specs=pl.BlockSpec((tile, two.shape[0]), lambda i: (i, 0)),
        out_shape=jax.ShapeDtypeStruct((rows, two.shape[0]), BF),
        compiler_params=ROOM,
        cost_estimate=LIGHT,
        name="far",
    )(one, two)


def product_near(one, two, got, span):
    width = two.shape[0]

    def kernel(left, right, more, *outs):
        values = lax.dot_general(left[...], right[...], NT, preferred_element_type=F32)
        block = (values + more[...].astype(F32)).astype(BF)
        put_split(pl.program_id(0), width // 2, block, *outs)

    return pl.pallas_call(
        kernel,
        grid=(one.shape[0] // 2 // span,),
        in_specs=[
            pl.BlockSpec((span, one.shape[1]), lambda i: (i, 0)),
            whole(two),
            pl.BlockSpec((span, width), lambda i: (i, 0)),
        ],
        out_specs=split_specs(span, width),
        out_shape=split_shapes(span, width),
        compiler_params=MORE_ROOM,
        cost_estimate=LIGHT,
        name="near",
    )(one, two, got)


def share_kernel(near, qkv, qkv_weight, hidden, weight, gain_one, gain_two, normed, *rest):
    outs, sums = rest[-5:-1] if near else rest[:1], rest[-1]
    one = lax.dot_general(qkv[...], qkv_weight[...], NT, preferred_element_type=F32)
    two = lax.dot_general(hidden[...], weight[...], NT, preferred_element_type=F32)
    scaled = normed[...].astype(F32)

    @pl.when(pl.program_id(0) == 0)
    def clear():
        sums[...] = jnp.zeros_like(sums)

    for row, values in enumerate((one * scaled, one, two * scaled, two)):
        sums[row : row + 1, :] += jnp.sum(values, axis=0, keepdims=True)
    share = one * gain_one[...] + two * gain_two[...]
    if near:
        block = (share + rest[0][...].astype(F32)).astype(BF)
        put_split(pl.program_id(0), share.shape[1] // 2, block, *outs)
    else:
        outs[0][...] = share.astype(BF)


def shares(near, qkv, qkv_weight, hidden, weight, gains, normed, span, got=None):
    rows, width = normed.shape
    steps = rows // 2 // span
    offset = 0 if near else steps

    def rows_of(array):
        return pl.BlockSpec((span, array.shape[1]), lambda i: (i + offset, 0))

    extra = [got] if near else []
    block = pl.BlockSpec((span, width), lambda i: (i, 0))
    return pl.pallas_call(
        functools.partial(share_kernel, near),
        grid=(steps,),
        in_specs=[
            rows_of(qkv),
            whole(qkv_weight),
            rows_of(hidden),
            whole(weight),
            whole(gains[0]),
            whole(gains[1]),
            rows_of(normed),
        ]
        + [block] * len(extra),
        out_specs=(split_specs(span, width) if near else [block])
        + [pl.BlockSpec((8, width), lambda i: (0, 0))],
        out_shape=(
            split_shapes(span, width) if near else [jax.ShapeDtypeStruct((rows // 2, width), BF)]
        )
        + [jax.ShapeDtypeStruct((8, width), F32)],
        compiler_params=MORE_ROOM,
        cost_estimate=LIGHT,
        name="share_near" if near else "share_far",
    )(qkv, qkv_weight, hidden, weight, *gains, normed, *extra)


def norm_kernel(near, far, gain_one, bias_one, gain_two, bias_two, normed, attn_in, mlp_in):
    half = pl.num_programs(0) // 2

    def write(block):
        values = block[...].astype(F32)
        centred = values - jnp.mean(values, axis=1, keepdims=True)
        spread = jnp.mean(centred * centred, axis=1, keepdims=True)
        scaled = centred * lax.rsqrt(spread + NORM_EPS)
        normed[...] = scaled.astype(BF)
        attn_in[...] = (scaled * gain_one[...] + bias_one[...]).astype(BF)
        mlp_in[...] = (scaled * gain_two[...] + bias_two[...]).astype(BF)

    pl.when(pl.program_id(0) < half)(lambda: write(near))
    pl.when(pl.program_id(0) >= half)(lambda: write(far))


def norms(near, far, span, *vectors):
    rows, width = near.shape
    half = rows // span
    vector = pl.BlockSpec((1, width), lambda i: (0, 0))
    block = pl.BlockSpec((span, width), lambda i: (i, 0))
    return pl.pallas_call(
        norm_kernel,
        grid=(2 * half,),
        in_specs=[
            pl.BlockSpec((span, width), lambda i: (jnp.minimum(i, half - 1), 0)),
            pl.BlockSpec((span, width), lambda i: (jnp.maximum(i - half, 0), 0)),
        ]
        + [vector] * 4,
        out_specs=[block] * 3,
        out_shape=[jax.ShapeDtypeStruct((2 * rows, width), BF)] * 3,
        compiler_params=ROOM,
        cost_estimate=LIGHT,
        name="norms",
    )(near, far, *[v.astype(F32)[None, :] for v in vectors])


def join_kernel(own, one, two, low, high, out):
    half = low.shape[0]
    for index, source in enumerate((own, one, two)):

        @pl.when(pl.program_id(0) == index)
        def copy(source=source):
            out[...] = source[...]

    @pl.when(pl.program_id(0) == 3)
    def last():
        out[:half, :] = low[...]
        out[half:, :] = high[...]


def join(*pieces):
    rows, width = pieces[0].shape
    return pl.pallas_call(
        join_kernel,
        grid=(4,),
        in_specs=[whole(piece) for piece in pieces],
        out_specs=pl.BlockSpec((rows, width), lambda i: (i, 0)),
        out_shape=jax.ShapeDtypeStruct((4 * rows, width), BF),
        compiler_params=ROOM,
        cost_estimate=LIGHT,
        name="join",
    )(*pieces)


def columns_kernel(places, values, near, far, out):
    count = pl.num_programs(0) // 2

    def write(source):
        out[...] = jnp.dot(values[...], source[...], preferred_element_type=F32)

    pl.when(pl.program_id(0) < count)(lambda: write(near))
    pl.when(pl.program_id(0) >= count)(lambda: write(far))


def columns_product(values, near, far, places):
    count = lax.axis_size("head")
    rows, depth = values.shape
    width = near.shape[1]
    return pl.pallas_call(
        columns_kernel,
        grid_spec=pltpu.PrefetchScalarGridSpec(
            num_scalar_prefetch=1,
            grid=(2 * count,),
            in_specs=[
                pl.BlockSpec((rows, depth), lambda r, p: (0, 0)),
                pl.BlockSpec((depth, width), lambda r, p: (jnp.minimum(r, count - 1), 0)),
                pl.BlockSpec((depth, width), lambda r, p: (jnp.maximum(r - count, 0), 0)),
            ],
            out_specs=pl.BlockSpec((rows, width), lambda r, p: (0, p[r])),
        ),
        out_shape=jax.ShapeDtypeStruct((rows, 2 * count * width), F32),
        compiler_params=ROOM,
        cost_estimate=LIGHT,
        name="columns",
    )(places, values, near, far)


def spread_kernel(parts, places, near, far, *outs):
    count = near.shape[0]
    each = near.shape[2] // sum(parts)
    for relative in range(2 * count):
        source = near if relative < count else far
        at = 0
        for out, part in zip(outs, parts):
            for index in range(part):
                where = (index * 2 * count + places[relative]) * each
                out[:, pl.ds(pl.multiple_of(where, each), each)] = source[
                    relative % count, :, at * each : (at + 1) * each
                ].astype(F32)
                at += 1


def spread_columns(near, far, places, parts):
    count = lax.axis_size("head")
    rows = near.shape[0] // count
    width = near.shape[1]
    step = min(rows, 64)
    each = width // sum(parts)
    taken = pl.BlockSpec((count, step, width), lambda i, p: (0, i, 0))
    wide = [2 * count * each * part for part in parts]
    return pl.pallas_call(
        functools.partial(spread_kernel, parts),
        grid_spec=pltpu.PrefetchScalarGridSpec(
            num_scalar_prefetch=1,
            grid=(rows // step,),
            in_specs=[taken, taken],
            out_specs=[pl.BlockSpec((step, w), lambda i, p: (i, 0)) for w in wide],
        ),
        out_shape=[jax.ShapeDtypeStruct((rows, w), F32) for w in wide],
        compiler_params=ROOM,
        cost_estimate=LIGHT,
        name="spread",
    )(places, near.reshape(count, rows, width), far.reshape(count, rows, width))


def place_kernel(places, blocks, *rest):
    rest[-1][...] = blocks[...].astype(F32)


def place_blocks(blocks, places, begun=None):
    count = lax.axis_size("head")
    rows, width = blocks.shape[0] // count, blocks.shape[1]
    extra = () if begun is None else (begun,)
    return pl.pallas_call(
        place_kernel,
        grid_spec=pltpu.PrefetchScalarGridSpec(
            num_scalar_prefetch=1,
            grid=(count,),
            in_specs=[pl.BlockSpec((rows, width), lambda r, p: (r, 0))]
            + [pl.BlockSpec(memory_space=pl.ANY) for _ in extra],
            out_specs=pl.BlockSpec((rows, width), lambda r, p: (0, p[r])),
        ),
        out_shape=jax.ShapeDtypeStruct((rows, 2 * count * width), F32),
        input_output_aliases={2: 0} if extra else {},
        compiler_params=ROOM,
        cost_estimate=LIGHT,
        name="place",
    )(places, blocks, *extra)


def turn(values, cosine, sine):
    low = values[:, : cosine.shape[1]]
    lane = lax.broadcasted_iota(jnp.int32, low.shape, 1)
    half = ROT // 2
    partner = jnp.where(
        lane < half, pltpu.roll(low, low.shape[1] - half, 1), pltpu.roll(low, half, 1)
    )
    return jnp.concatenate([low * cosine + partner * sine, values[:, cosine.shape[1] :]], axis=1)


def attention_kernel(
    order, first, qkv, bias, upstream, cosine, sine, context, context_rel, grads, keys, values,
    score, prob_grad, key_sum, value_sum,
):
    step = pl.program_id(0)
    total = pl.num_programs(0)
    size = HEAD_SIZE
    span = qkv.shape[1]
    last = (((1,), (1,)), ((), ()))
    rows = (((0,), (0,)), ((), ()))
    mine = order[step]
    start = first[step]
    cos_here, sin_here = cosine[mine], sine[mine]
    joined = qkv[0].astype(F32) + bias[...]
    query = (turn(joined[:, :size], cos_here, sin_here) * (size**-0.5)).astype(BF)
    at = pl.ds(pl.multiple_of(step * span, span), span)
    keys[at, :] = turn(joined[:, size : 2 * size], cos_here, sin_here).astype(BF)
    values[at, :] = joined[:, 2 * size :].astype(BF)
    key_sum[at, :] = jnp.zeros((span, size), F32)
    value_sum[at, :] = jnp.zeros((span, size), F32)
    up = upstream[0]

    def one(count):
        blocks = [slice(i * span, (i + 1) * span) for i in range(count)]
        top = jnp.full((span, 1), NEG_FILL, F32)
        for i, block in enumerate(blocks):
            part = lax.dot_general(query, keys[block, :], last, preferred_element_type=F32)
            if i == count - 1:
                row = lax.broadcasted_iota(jnp.int32, part.shape, 0)
                column = lax.broadcasted_iota(jnp.int32, part.shape, 1)
                part = jnp.where(column <= row, part, NEG_FILL)
            else:
                part = part + jnp.where(i >= start, 0.0, NEG_FILL)
            score[:, block] = part
            top = jnp.maximum(top, jnp.max(part, axis=1, keepdims=True))
        norm = jnp.zeros((span, 1), F32)
        for block in blocks:
            part = jnp.exp(score[:, block] - top)
            score[:, block] = part
            norm = norm + jnp.sum(part, axis=1, keepdims=True)
        inverse = 1.0 / norm
        out = jnp.zeros((span, size), F32)
        inner = jnp.zeros((span, 1), F32)
        for block in blocks:
            probs = score[:, block] * inverse
            score[:, block] = probs
            grad = lax.dot_general(up, values[block, :], last, preferred_element_type=F32)
            prob_grad[:, block] = grad
            inner = inner + jnp.sum(probs * grad, axis=1, keepdims=True)
            low = probs.astype(BF)
            out = out + jnp.dot(low, values[block, :], preferred_element_type=F32)
            value_sum[block, :] += lax.dot_general(low, up, rows, preferred_element_type=F32)
        context[0] = out.astype(BF)
        context_rel[0] = out.astype(BF)
        query_grad = jnp.zeros((span, size), F32)
        for block in blocks:
            low = (score[:, block] * (prob_grad[:, block] - inner)).astype(BF)
            query_grad = query_grad + jnp.dot(low, keys[block, :], preferred_element_type=F32)
            key_sum[block, :] += lax.dot_general(low, query, rows, preferred_element_type=F32)
        query_grad = (query_grad * (size**-0.5)).astype(BF).astype(F32)
        grads[mine, :, :size] = turn(query_grad, cos_here, -sin_here).astype(BF)

    steps = keys.shape[0] // span
    for index in range(steps):
        pl.when(step == index)(functools.partial(one, index + 1))

    @pl.when(step == total - 1)
    def finish():
        def each(index, carry):
            place = order[index]
            block = pl.ds(pl.multiple_of(index * span, span), span)
            key_grad = key_sum[block, :].astype(BF).astype(F32)
            grads[place, :, size : 2 * size] = turn(key_grad, cosine[place], -sine[place]).astype(
                BF
            )
            grads[place, :, 2 * size :] = value_sum[block, :].astype(BF)
            return carry

        lax.fori_loop(0, total, each, 0)


def attention(order, first, qkv, bias, upstream, cosine, sine):
    count, span, width = qkv.shape
    size = HEAD_SIZE
    length = count * span
    whole = lambda *shape: pl.BlockSpec(shape, lambda i, o, f: (0,) * len(shape))
    taken = lambda *shape: pl.BlockSpec(
        (1,) + shape, lambda i, o, f: (o[i],) + (0,) * len(shape)
    )
    pairs = count * (count + 1) // 2
    return pl.pallas_call(
        attention_kernel,
        grid_spec=pltpu.PrefetchScalarGridSpec(
            num_scalar_prefetch=2,
            grid=(count,),
            in_specs=[
                taken(span, width),
                whole(1, width),
                taken(span, size),
                whole(count, span, cosine.shape[-1]),
                whole(count, span, cosine.shape[-1]),
            ],
            out_specs=[
                pl.BlockSpec((1, span, size), lambda i, o, f: (i, 0, 0)),
                taken(span, size),
                whole(count, span, width),
            ],
            scratch_shapes=[
                pltpu.VMEM((length, size), BF),
                pltpu.VMEM((length, size), BF),
                pltpu.VMEM((span, length), F32),
                pltpu.VMEM((span, length), F32),
                pltpu.VMEM((length, size), F32),
                pltpu.VMEM((length, size), F32),
            ],
        ),
        out_shape=[
            jax.ShapeDtypeStruct((count, span, size), BF),
            jax.ShapeDtypeStruct((count, span, size), BF),
            jax.ShapeDtypeStruct((count, span, width), BF),
        ],
        compiler_params=ROOM,
        cost_estimate=LIGHT,
        name="attention",
    )(order, first, qkv, bias, upstream, cosine, sine)


def segment_start(lengths, at):
    lengths = lengths.reshape(-1)
    starts = jnp.stack([jnp.sum(lengths[:i]) for i in range(lengths.shape[0])])
    return jnp.max(jnp.where(starts[None, :] <= at[:, None], starts[None, :], 0), axis=1).astype(
        jnp.int32
    )


def rotary_tables(lengths, places, span):
    at = places * span
    offset = (at - segment_start(lengths, at))[:, None] + jnp.arange(span, dtype=jnp.int32)[None, :]
    half = ROT // 2
    frequency = ROT_BASE ** (-(2.0 * jnp.arange(half, dtype=F32)) / ROT)
    angles = offset.astype(F32)[..., None] * frequency
    cosine, sine = jnp.cos(angles), jnp.sin(angles)
    rest = jnp.zeros(offset.shape + (128 - ROT,), F32)
    return (
        jnp.concatenate([cosine, cosine, rest + 1.0], axis=-1),
        jnp.concatenate([-sine, sine, rest], axis=-1),
    )


def body(
    block_in,
    cotangent,
    seg_lengths,
    ln1_gain,
    ln1_bias,
    qkv_weight,
    qkv_bias,
    out_weight,
    out_bias,
    ln2_gain,
    ln2_bias,
    fc1_weight,
    fc1_bias,
    fc2_weight,
    fc2_bias,
):
    rows_here, span, width = block_in.shape
    shard, hidden_units = fc1_weight.shape
    data_count = lax.axis_size("dp")
    head_count = lax.axis_size("head")
    blk_count = lax.axis_size("blk")
    plane = head_count * blk_count
    head_place = lax.axis_index("head")
    blk_place = lax.axis_index("blk")
    place = head_place * blk_count + blk_place
    each = hidden_units // plane
    length = plane * span

    places = [
        (head_place ^ (r % head_count)) * blk_count + (blk_place ^ (r // head_count))
        for r in range(plane)
    ]
    place_list = jnp.stack(places).astype(jnp.int32)
    absolute = jnp.arange(plane, dtype=jnp.int32)
    order = (absolute % blk_count ^ blk_place) * head_count + (absolute // blk_count ^ head_place)

    def columns(values, wide):
        return lax.dynamic_slice_in_dim(values, place * wide, wide, 1)

    own_in = block_in.reshape(span, width)
    own_up = cotangent.reshape(span, width)
    out_shard = columns(out_weight, HEAD_SIZE)
    qkv_shard = jnp.concatenate(
        [
            columns(qkv_weight[:, part * width : (part + 1) * width], HEAD_SIZE)
            for part in range(3)
        ],
        axis=1,
    )
    out_shard, own_in = tie(out_shard, own_in)
    out_mine = data_gather(out_shard)
    tokens_begun = gather_start(own_in)
    tokens_begun, own_up, qkv_shard = tie(tokens_begun, own_up, qkv_shard)
    qkv_mine = data_gather(qkv_shard)
    upstream_begun = gather_start(own_up)
    tokens_near, tokens_far = gather_end(*gather_middle(*tokens_begun))
    fc1_shard, tokens_near = tie(columns(fc1_weight, each), tokens_near)
    fc1_mine = data_gather(fc1_shard)
    cosine, sine = rotary_tables(seg_lengths, jnp.stack(places), span)
    normed, attn_in, mlp_in = norms(
        tokens_near, tokens_far, span, ln1_gain, ln1_bias, ln2_gain, ln2_bias
    )
    upstream_begun, attn_in, cosine, sine, out_mine = tie(
        upstream_begun, attn_in, cosine, sine, out_mine
    )
    out_rows = lax.all_to_all(out_mine, ("head", "blk"), split_axis=0, concat_axis=1, tiled=True)
    upstream_near, upstream_far = gather_end(*gather_middle(*upstream_begun))
    upstream_near, qkv_mine, attn_in = tie(upstream_near, qkv_mine, attn_in)

    first = segment_start(seg_lengths, absolute * span) // span

    joined = product(attn_in, qkv_mine, NN, kind=F32)
    upstream_near, upstream_far, joined, out_rows = tie(
        upstream_near, upstream_far, joined, out_rows
    )
    upstream = jnp.concatenate([upstream_near, upstream_far], axis=0)
    context_grad = product(upstream, out_rows, NT)
    bias_mine = jnp.concatenate(
        [
            lax.dynamic_slice_in_dim(qkv_bias, part * width + place * HEAD_SIZE, HEAD_SIZE, 0)
            for part in range(3)
        ]
    ).astype(F32)
    context_abs, context, qkv_grad = attention(
        order.astype(jnp.int32),
        first,
        joined.reshape(plane, span, 3 * HEAD_SIZE),
        bias_mine[None, :],
        context_grad.reshape(plane, span, HEAD_SIZE),
        cosine,
        sine,
    )
    context = context.reshape(length, HEAD_SIZE)
    qkv_grad = qkv_grad.reshape(length, 3 * HEAD_SIZE)
    out_grad = wide_product(context, upstream)
    out_grad = lax.all_to_all(out_grad, ("head", "blk"), split_axis=1, concat_axis=0, tiled=True)
    qkv_w_grad = product(attn_in, qkv_grad, TN)
    att_grad = jnp.concatenate([qkv_w_grad, out_grad], axis=1)

    fc1_mine, att_grad, context_abs, out_mine, fc2_shard = tie(
        fc1_mine, att_grad, context_abs, out_mine, columns(fc2_weight, each)
    )
    chain = data_count == 4
    if chain:
        move_one = exchange_one(fc2_shard, att_grad)
    else:
        fc2_mine, att_sum = data_gather(fc2_shard), data_scatter(att_grad)
    out_moved = gather_start(out_mine)
    fc1_bias_mine = lax.dynamic_slice_in_dim(fc1_bias, place * each, each, 0).astype(F32)
    active, slope = hidden_units_of(mlp_in, fc1_mine, fc1_bias_mine[None, :])
    if chain:
        move_one, out_moved, fc2_shard, att_grad, active = tie(
            move_one, out_moved, fc2_shard, att_grad, active
        )
        move_two = exchange_two(fc2_shard, att_grad, *move_one)
    out_moved = gather_middle(*out_moved)
    fc2_grad = product(upstream, active, TN)
    if chain:
        move_two, out_moved, att_grad, fc2_grad, context_abs = tie(
            move_two, out_moved, att_grad, fc2_grad, context_abs
        )
        move_three = exchange_three(att_grad, *move_two)
    own_context = lax.all_to_all(
        context_abs.reshape(length, HEAD_SIZE),
        ("head", "blk"),
        split_axis=0,
        concat_axis=1,
        tiled=True,
    )
    if chain:
        move_three, att_grad, own_context, out_moved = tie(
            move_three, att_grad, own_context, out_moved
        )
        move_four = exchange_four(att_grad, *move_three)
    if chain:
        move_four, fc2_grad = tie(move_four, fc2_grad)
        att_sum, fc2_mine = exchange_end(
            fc2_shard, att_grad, move_one, move_two, move_three, move_four
        )
    fc2_sum = data_scatter(fc2_grad)

    att_moved = gather_start(att_sum)
    mlp_far = product_far(active, fc2_mine)
    mlp_got = other_core(mlp_far)
    hidden_grad, fc1_bias_part = hidden_grad_of(upstream, fc2_mine, slope)
    att_moved, mlp_got, hidden_grad, active = tie(att_moved, mlp_got, hidden_grad, active)
    att_moved = gather_middle(*att_moved)
    mlp_parts = product_near(active, fc2_mine, mlp_got, span)
    att_moved, mlp_parts, hidden_grad = tie(att_moved, mlp_parts, hidden_grad)
    mlp_got = collect_start(*mlp_parts)
    fc1_grad = product(mlp_in, hidden_grad, TN)
    att_near, out_near = join(*att_moved), join(*out_moved)
    mlp_got, fc1_grad, hidden_grad, fc2_sum, att_near, out_near = tie(
        mlp_got, fc1_grad, hidden_grad, fc2_sum, att_near, out_near
    )
    fc1_sum = data_scatter(fc1_grad)
    mlp_done = collect_middle(mlp_parts, mlp_got)
    att_far, out_far = other_core(att_near), other_core(out_near)
    gains = (ln1_gain.astype(F32)[None, :], ln2_gain.astype(F32)[None, :])
    share_far, sums_far = shares(
        False, qkv_grad, qkv_mine, hidden_grad, fc1_mine, gains, normed, span
    )
    mlp_done, share_far, att_far, out_far, fc2_sum = tie(
        mlp_done, share_far, att_far, out_far, fc2_sum
    )
    share_got = other_core(share_far)
    fc2_moved = gather_start(fc2_sum)
    *share_parts, sums_near = shares(
        True, qkv_grad, qkv_mine, hidden_grad, fc1_mine, gains, normed, span, share_got
    )
    fc2_moved, share_parts, att_far, out_far = tie(fc2_moved, share_parts, att_far, out_far)
    share_got = collect_start(*share_parts)
    fc2_moved = gather_middle(*fc2_moved)
    attn_out = columns_product(own_context, out_near, out_far, place_list) + out_bias
    qkv_out, out_out = spread_columns(att_near, att_far, place_list, (3, 1))
    mlp_out = collect_end(*mlp_done) + fc2_bias
    own_float = own_in.astype(F32)
    block_out = (own_float + attn_out + mlp_out).astype(BF).reshape(block_in.shape)

    moves = sum_moves()
    qkv_bias_part = jnp.sum(qkv_grad.astype(F32), axis=0).reshape(3, 1, HEAD_SIZE)
    here = (jnp.arange(plane) == place).astype(F32)
    norm_sums = sums_far + sums_near
    terms = (
        norm_sums[0],
        norm_sums[1],
        (qkv_bias_part * here[None, :, None]).reshape(-1),
        jnp.sum(own_up.astype(F32), axis=0),
        norm_sums[2],
        norm_sums[3],
        (here[:, None] * fc1_bias_part).reshape(-1),
        jnp.stack([jnp.sum(attn_out * attn_out), jnp.sum(mlp_out * mlp_out)]),
    )
    sizes = [term.shape[0] for term in terms]
    vector = jnp.concatenate(terms + (jnp.zeros((-sum(sizes) % 1024,), F32),)).reshape(-1, 128)
    share_got, fc2_moved, vector, block_out, qkv_out, out_out, fc1_sum = tie(
        share_got, fc2_moved, vector, block_out, qkv_out, out_out, fc1_sum
    )
    share_done = collect_middle(share_parts, share_got)
    fc1_moved = gather_start(fc1_sum)
    vector = sum_move(sum_move(vector, moves[0]), moves[1])
    fc2_near = join(*fc2_moved)
    share_done, fc1_moved, vector, fc2_near = tie(share_done, fc1_moved, vector, fc2_near)
    fc1_moved = gather_middle(*fc1_moved)
    fc2_far = other_core(fc2_near)
    fc2_out = place_blocks(fc2_near, place_list[:head_count])
    vector = sum_move(vector, moves[2])

    share = collect_end(*share_done)
    own_centred = own_float - jnp.mean(own_float, axis=-1, keepdims=True)
    own_scaled = lax.rsqrt(jnp.mean(own_centred * own_centred, axis=-1, keepdims=True) + NORM_EPS)
    own_normed = own_centred * own_scaled
    share = own_scaled * (
        share
        - jnp.mean(share, axis=-1, keepdims=True)
        - own_normed * jnp.mean(share * own_normed, axis=-1, keepdims=True)
    )
    input_grad = (own_up.astype(F32) + share).astype(BF).reshape(block_in.shape)

    fc1_moved, vector, fc2_out, fc2_far, input_grad = tie(
        fc1_moved, vector, fc2_out, fc2_far, input_grad
    )
    fc1_near, fc1_far = gather_end(*fc1_moved)
    fc2_out = place_blocks(fc2_far, place_list[head_count:], fc2_out)
    fc1_out = place_blocks(fc1_near, place_list[:head_count])
    for move in moves[3:]:
        vector = sum_move(vector, move)
    fc1_far, fc1_out, fc2_out, vector = tie(fc1_far, fc1_out, fc2_out, vector)
    fc1_out = place_blocks(fc1_far, place_list[head_count:], fc1_out)
    reduced = [
        vector.reshape(-1)[sum(sizes[:i]) : sum(sizes[: i + 1])] for i in range(len(sizes))
    ]
    entries = rows_here * length * data_count * width
    branch_rms = jnp.sqrt(reduced[7] / entries)
    return (
        block_out,
        input_grad,
        reduced[0],
        reduced[1],
        qkv_out,
        reduced[2],
        out_out,
        reduced[3],
        reduced[4],
        reduced[5],
        fc1_out,
        reduced[6],
        fc2_out,
        reduced[3],
        branch_rms[0],
        branch_rms[1],
    )


def solution(mesh):
    rows, tokens, whole = P("dp", None), P("dp", ("head", "blk"), None), P()
    return jax.shard_map(
        body,
        mesh=mesh,
        in_specs=(
            tokens,
            tokens,
            rows,
            whole,
            whole,
            rows,
            whole,
            rows,
            whole,
            whole,
            whole,
            rows,
            whole,
            rows,
            whole,
        ),
        out_specs=(
            tokens,
            tokens,
            whole,
            whole,
            rows,
            whole,
            rows,
            whole,
            whole,
            whole,
            rows,
            whole,
            rows,
            whole,
            whole,
            whole,
        ),
        check_vma=False,
    )
```

```python
import functools

import jax
import jax.numpy as jnp
from jax import lax
from jax.experimental import pallas as pl
from jax.experimental.pallas import tpu as pltpu
from jax.sharding import PartitionSpec as P

HEADS = 8
HEAD_SIZE = 256
ROT = 64
NORM_EPS = 1e-05
NEG_FILL = -1e30
ROT_BASE = 10000.0
BF = jnp.bfloat16
F32 = jnp.float32
NN = (((1,), (0,)), ((), ()))
NT = (((1,), (1,)), ((), ()))
TN = (((0,), (0,)), ((), ()))
LIGHT = pl.CostEstimate(flops=10**9, bytes_accessed=10**6, transcendentals=0)
ROOM = pltpu.CompilerParams(vmem_limit_bytes=48 * 2**20)
MORE_ROOM = pltpu.CompilerParams(vmem_limit_bytes=48 * 2**20)


def across(values, offset):
    count = lax.axis_size("head")
    return lax.ppermute(values, "head", [(i, i ^ offset) for i in range(count)])


def other_core(values):
    return lax.ppermute(values, "blk", [(0, 1), (1, 0)])


def tie(*trees):
    leaves, form = jax.tree.flatten(trees)
    return jax.tree.unflatten(form, lax.optimization_barrier(leaves))


def gather_start(own):
    return own, across(own, 1), across(own, 2)


def gather_middle(own, one, two):
    half = own.shape[0] // 2
    return own, one, two, across(one[:half], 2), across(two[half:], 1)


def gather_end(*pieces):
    near = join(*pieces)
    return near, other_core(near)


def data_gather(own):
    return lax.all_gather(own, "dp", axis=0, tiled=True)


def data_scatter(partial):
    return lax.psum_scatter(partial, "dp", scatter_dimension=0, tiled=True)


def hop_up(values):
    return lax.ppermute(values, "dp", [(0, 1), (1, 2), (2, 3)])


def hop_down(values):
    return lax.ppermute(values, "dp", [(3, 2), (2, 1), (1, 0)])


def part_of(sums, index):
    rows = sums.shape[0] // 4
    return lax.dynamic_slice_in_dim(sums, index * rows, rows, 0)


def exchange_one(own, sums):
    place = lax.axis_index("dp")
    return (
        hop_up(jnp.where(place == 0, part_of(sums, 3), own)),
        hop_down(jnp.where(place == 3, part_of(sums, 0), own)),
    )


def exchange_two(own, sums, up, down):
    place = lax.axis_index("dp")
    up = jnp.where(place == 0, own, jnp.where(place == 1, plus(part_of(sums, 3), up), up))
    down = jnp.where(place == 3, own, jnp.where(place == 2, plus(part_of(sums, 0), down), down))
    return hop_up(up), hop_down(down)


def exchange_three(sums, up, down):
    place = lax.axis_index("dp")
    more_up = plus(part_of(sums, 3), up)
    more_down = plus(part_of(sums, 0), down)
    up = jnp.where(place == 0, part_of(sums, 2), jnp.where(place == 2, more_up, up))
    down = jnp.where(place == 3, part_of(sums, 1), jnp.where(place == 1, more_down, down))
    return hop_up(up), hop_down(down)


def exchange_four(sums, up, down):
    place = lax.axis_index("dp")
    more_up = plus(part_of(sums, 2), up)
    more_down = plus(part_of(sums, 1), down)
    up = jnp.where(place == 0, part_of(sums, 1), jnp.where(place == 1, more_up, up))
    down = jnp.where(place == 3, part_of(sums, 2), jnp.where(place == 2, more_down, down))
    return hop_up(up), hop_down(down)


def exchange_end(own, sums, one, two, three, four):
    place = lax.axis_index("dp")
    rows = own.shape[0]

    def choose(*values):
        out = values[-1]
        for index in range(len(values) - 2, -1, -1):
            if values[index] is not out:
                out = jnp.where(place == index, values[index], out)
        return out

    first = choose(three[1], four[0], four[0], three[0]).astype(F32)
    inner = (place == 1) | (place == 2)
    second = jnp.where(inner, four[1].astype(F32), 0.0)
    total = part_of(sums, place).astype(F32) + first + second
    total, own, one, two, three, four = tie(total.astype(BF), own, one, two, three, four)
    up, down = 0, 1
    whole = jnp.zeros((4 * rows,) + own.shape[1:], own.dtype)
    for step, piece in enumerate(
        (
            own,
            jnp.where(place < 2, one[down], choose(two[down], two[down], two[down], four[up])),
            choose(two[down], three[down], three[up], two[up]),
            jnp.where(place >= 2, one[up], choose(four[down], two[up], two[up], two[up])),
        )
    ):
        whole = lax.dynamic_update_slice_in_dim(whole, piece, (place + step) % 4 * rows, 0)
    return total, whole


def plus(one, two):
    return (one.astype(F32) + two.astype(F32)).astype(BF)


def sum_moves():
    moves = []
    for axis in ("blk", "head", "dp"):
        count = lax.axis_size(axis)
        moves += [
            (axis, [(i, i ^ 2**k) for i in range(count)]) for k in range(count.bit_length() - 1)
        ]
    return moves


def sum_move(vector, move):
    return vector + lax.ppermute(vector, *move)


def whole(array):
    return pl.BlockSpec(array.shape, lambda i: (0,) * array.ndim)


def product(one, two, dims, tile=512, kind=BF):
    def kernel(left, right, out):
        out[...] = lax.dot_general(
            left[...], right[...], dims, preferred_element_type=F32
        ).astype(out.dtype)

    if dims == TN:
        rows, left_spec = one.shape[1], pl.BlockSpec((one.shape[0], tile), lambda i: (0, i))
    else:
        rows, left_spec = one.shape[0], pl.BlockSpec((tile, one.shape[1]), lambda i: (i, 0))
    columns = two.shape[0] if dims == NT else two.shape[1]
    return pl.pallas_call(
        kernel,
        grid=(rows // tile,),
        in_specs=[left_spec, whole(two)],
        out_specs=pl.BlockSpec((tile, columns), lambda i: (i, 0)),
        out_shape=jax.ShapeDtypeStruct((rows, columns), kind),
        compiler_params=ROOM,
        cost_estimate=LIGHT,
        name="product",
    )(one, two)


def wide_product(one, two, tile=512):
    def kernel(left, right, out):
        out[...] = lax.dot_general(
            left[...], right[...], TN, preferred_element_type=F32
        ).astype(BF)

    return pl.pallas_call(
        kernel,
        grid=(two.shape[1] // tile,),
        in_specs=[whole(one), pl.BlockSpec((two.shape[0], tile), lambda i: (0, i))],
        out_specs=pl.BlockSpec((one.shape[1], tile), lambda i: (0, i)),
        out_shape=jax.ShapeDtypeStruct((one.shape[1], two.shape[1]), BF),
        compiler_params=ROOM,
        cost_estimate=LIGHT,
        name="wide",
    )(one, two)


def hidden_kernel(tokens, weight, bias, active, slope):
    hidden = jnp.dot(tokens[...], weight[...], preferred_element_type=F32) + bias[...]
    phi = 0.5 * (1.0 + lax.erf(hidden * (0.5**0.5)))
    active[...] = (hidden * phi).astype(BF)
    density = jnp.exp(-0.5 * hidden * hidden) * ((2.0 * jnp.pi) ** -0.5)
    slope[...] = (phi + hidden * density).astype(BF)


def hidden_units_of(tokens, weight, bias, tile=512):
    rows, width = tokens.shape
    wide = weight.shape[1]
    out = pl.BlockSpec((tile, wide), lambda i: (i, 0))
    return pl.pallas_call(
        hidden_kernel,
        grid=(rows // tile,),
        in_specs=[pl.BlockSpec((tile, width), lambda i: (i, 0)), whole(weight), whole(bias)],
        out_specs=[out, out],
        out_shape=[jax.ShapeDtypeStruct((rows, wide), BF)] * 2,
        compiler_params=MORE_ROOM,
        cost_estimate=LIGHT,
        name="hidden",
    )(tokens, weight, bias)


def hidden_grad_kernel(upstream, weight, slope, grad, total):
    values = jnp.dot(upstream[...], weight[...], preferred_element_type=F32)
    low = (values * slope[...].astype(F32)).astype(BF)
    grad[...] = low

    @pl.when(pl.program_id(0) == 0)
    def clear():
        total[...] = jnp.zeros_like(total)

    total[...] += jnp.sum(low.astype(F32), axis=0, keepdims=True)


def hidden_grad_of(upstream, weight, slope, tile=512):
    rows, width = upstream.shape
    wide = weight.shape[1]
    out = pl.BlockSpec((tile, wide), lambda i: (i, 0))
    return pl.pallas_call(
        hidden_grad_kernel,
        grid=(rows // tile,),
        in_specs=[pl.BlockSpec((tile, width), lambda i: (i, 0)), whole(weight), out],
        out_specs=[out, pl.BlockSpec((1, wide), lambda i: (0, 0))],
        out_shape=[
            jax.ShapeDtypeStruct((rows, wide), BF),
            jax.ShapeDtypeStruct((1, wide), F32),
        ],
        compiler_params=MORE_ROOM,
        cost_estimate=LIGHT,
        name="hidden_grad",
    )(upstream, weight, slope)


def put_split(step, side, block, left_keep, left_send, right_keep, right_send):
    left, right = block[:, :side], block[:, side:]
    for index, out, at in ((0, left_keep, 0), (1, left_send, 0), (2, left_keep, 1), (3, left_send, 1)):

        @pl.when(step == index)
        def write_left(out=out, at=at):
            out[at] = left

    for index, out, at in ((0, right_keep, 0), (1, right_keep, 1), (2, right_send, 0), (3, right_send, 1)):

        @pl.when(step == index)
        def write_right(out=out, at=at):
            out[at] = right


def split_shapes(span, width):
    return [jax.ShapeDtypeStruct((2, span, width // 2), BF)] * 4


def split_specs(span, width):
    return [pl.BlockSpec((2, span, width // 2), lambda i: (0, 0, 0))] * 4


def collect_start(left_keep, left_send, right_keep, right_send):
    return across(left_send, 1), across(right_send, 2)


def collect_middle(parts, got):
    (left_keep, _, right_keep, _), (left, right) = parts, got
    left_last = across(plus(left_keep[1], left[1]), 2)
    right_last = across(plus(right_keep[1], right[1]), 1)
    return (left_keep[0], left[0], left_last), (right_keep[0], right[0], right_last)


def collect_end(*sides):
    return jnp.concatenate(
        [sum(term.astype(F32) for term in terms[1:]) + terms[0].astype(F32) for terms in sides],
        axis=1,
    )


def product_far(one, two, tile=512):
    rows = one.shape[0] // 2

    def kernel(left, right, out):
        out[...] = lax.dot_general(
            left[...], right[...], NT, preferred_element_type=F32
        ).astype(BF)

    return pl.pallas_call(
        kernel,
        grid=(rows // tile,),
        in_specs=[
            pl.BlockSpec((tile, one.shape[1]), lambda i: (i + rows // tile, 0)),
            whole(two),
        ],
        out_specs=pl.BlockSpec((tile, two.shape[0]), lambda i: (i, 0)),
        out_shape=jax.ShapeDtypeStruct((rows, two.shape[0]), BF),
        compiler_params=ROOM,
        cost_estimate=LIGHT,
        name="far",
    )(one, two)


def product_near(one, two, got, span):
    width = two.shape[0]

    def kernel(left, right, more, *outs):
        values = lax.dot_general(left[...], right[...], NT, preferred_element_type=F32)
        block = (values + more[...].astype(F32)).astype(BF)
        put_split(pl.program_id(0), width // 2, block, *outs)

    return pl.pallas_call(
        kernel,
        grid=(one.shape[0] // 2 // span,),
        in_specs=[
            pl.BlockSpec((span, one.shape[1]), lambda i: (i, 0)),
            whole(two),
            pl.BlockSpec((span, width), lambda i: (i, 0)),
        ],
        out_specs=split_specs(span, width),
        out_shape=split_shapes(span, width),
        compiler_params=MORE_ROOM,
        cost_estimate=LIGHT,
        name="near",
    )(one, two, got)


def share_kernel(near, qkv, qkv_weight, hidden, weight, gain_one, gain_two, normed, *rest):
    outs, sums = rest[-5:-1] if near else rest[:1], rest[-1]
    one = lax.dot_general(qkv[...], qkv_weight[...], NT, preferred_element_type=F32)
    two = lax.dot_general(hidden[...], weight[...], NT, preferred_element_type=F32)
    scaled = normed[...].astype(F32)

    @pl.when(pl.program_id(0) == 0)
    def clear():
        sums[...] = jnp.zeros_like(sums)

    for row, values in enumerate((one * scaled, one, two * scaled, two)):
        sums[row : row + 1, :] += jnp.sum(values, axis=0, keepdims=True)
    share = one * gain_one[...] + two * gain_two[...]
    if near:
        block = (share + rest[0][...].astype(F32)).astype(BF)
        put_split(pl.program_id(0), share.shape[1] // 2, block, *outs)
    else:
        outs[0][...] = share.astype(BF)


def shares(near, qkv, qkv_weight, hidden, weight, gains, normed, span, got=None):
    rows, width = normed.shape
    steps = rows // 2 // span
    offset = 0 if near else steps

    def rows_of(array):
        return pl.BlockSpec((span, array.shape[1]), lambda i: (i + offset, 0))

    extra = [got] if near else []
    block = pl.BlockSpec((span, width), lambda i: (i, 0))
    return pl.pallas_call(
        functools.partial(share_kernel, near),
        grid=(steps,),
        in_specs=[
            rows_of(qkv),
            whole(qkv_weight),
            rows_of(hidden),
            whole(weight),
            whole(gains[0]),
            whole(gains[1]),
            rows_of(normed),
        ]
        + [block] * len(extra),
        out_specs=(split_specs(span, width) if near else [block])
        + [pl.BlockSpec((8, width), lambda i: (0, 0))],
        out_shape=(
            split_shapes(span, width) if near else [jax.ShapeDtypeStruct((rows // 2, width), BF)]
        )
        + [jax.ShapeDtypeStruct((8, width), F32)],
        compiler_params=MORE_ROOM,
        cost_estimate=LIGHT,
        name="share_near" if near else "share_far",
    )(qkv, qkv_weight, hidden, weight, *gains, normed, *extra)


def norm_kernel(near, far, gain_one, bias_one, gain_two, bias_two, normed, attn_in, mlp_in):
    half = pl.num_programs(0) // 2

    def write(block):
        values = block[...].astype(F32)
        centred = values - jnp.mean(values, axis=1, keepdims=True)
        spread = jnp.mean(centred * centred, axis=1, keepdims=True)
        scaled = centred * lax.rsqrt(spread + NORM_EPS)
        normed[...] = scaled.astype(BF)
        attn_in[...] = (scaled * gain_one[...] + bias_one[...]).astype(BF)
        mlp_in[...] = (scaled * gain_two[...] + bias_two[...]).astype(BF)

    pl.when(pl.program_id(0) < half)(lambda: write(near))
    pl.when(pl.program_id(0) >= half)(lambda: write(far))


def norms(near, far, span, *vectors):
    rows, width = near.shape
    half = rows // span
    vector = pl.BlockSpec((1, width), lambda i: (0, 0))
    block = pl.BlockSpec((span, width), lambda i: (i, 0))
    return pl.pallas_call(
        norm_kernel,
        grid=(2 * half,),
        in_specs=[
            pl.BlockSpec((span, width), lambda i: (jnp.minimum(i, half - 1), 0)),
            pl.BlockSpec((span, width), lambda i: (jnp.maximum(i - half, 0), 0)),
        ]
        + [vector] * 4,
        out_specs=[block] * 3,
        out_shape=[jax.ShapeDtypeStruct((2 * rows, width), BF)] * 3,
        compiler_params=ROOM,
        cost_estimate=LIGHT,
        name="norms",
    )(near, far, *[v.astype(F32)[None, :] for v in vectors])


def join_kernel(own, one, two, low, high, out):
    half = low.shape[0]
    for index, source in enumerate((own, one, two)):

        @pl.when(pl.program_id(0) == index)
        def copy(source=source):
            out[...] = source[...]

    @pl.when(pl.program_id(0) == 3)
    def last():
        out[:half, :] = low[...]
        out[half:, :] = high[...]


def join(*pieces):
    rows, width = pieces[0].shape
    return pl.pallas_call(
        join_kernel,
        grid=(4,),
        in_specs=[whole(piece) for piece in pieces],
        out_specs=pl.BlockSpec((rows, width), lambda i: (i, 0)),
        out_shape=jax.ShapeDtypeStruct((4 * rows, width), BF),
        compiler_params=ROOM,
        cost_estimate=LIGHT,
        name="join",
    )(*pieces)


def columns_kernel(places, values, near, far, out):
    count = pl.num_programs(0) // 2

    def write(source):
        out[...] = jnp.dot(values[...], source[...], preferred_element_type=F32)

    pl.when(pl.program_id(0) < count)(lambda: write(near))
    pl.when(pl.program_id(0) >= count)(lambda: write(far))


def columns_product(values, near, far, places):
    count = lax.axis_size("head")
    rows, depth = values.shape
    width = near.shape[1]
    return pl.pallas_call(
        columns_kernel,
        grid_spec=pltpu.PrefetchScalarGridSpec(
            num_scalar_prefetch=1,
            grid=(2 * count,),
            in_specs=[
                pl.BlockSpec((rows, depth), lambda r, p: (0, 0)),
                pl.BlockSpec((depth, width), lambda r, p: (jnp.minimum(r, count - 1), 0)),
                pl.BlockSpec((depth, width), lambda r, p: (jnp.maximum(r - count, 0), 0)),
            ],
            out_specs=pl.BlockSpec((rows, width), lambda r, p: (0, p[r])),
        ),
        out_shape=jax.ShapeDtypeStruct((rows, 2 * count * width), F32),
        compiler_params=ROOM,
        cost_estimate=LIGHT,
        name="columns",
    )(places, values, near, far)


def spread_kernel(parts, places, near, far, *outs):
    count = near.shape[0]
    each = near.shape[2] // sum(parts)
    for relative in range(2 * count):
        source = near if relative < count else far
        at = 0
        for out, part in zip(outs, parts):
            for index in range(part):
                where = (index * 2 * count + places[relative]) * each
                out[:, pl.ds(pl.multiple_of(where, each), each)] = source[
                    relative % count, :, at * each : (at + 1) * each
                ].astype(F32)
                at += 1


def spread_columns(near, far, places, parts):
    count = lax.axis_size("head")
    rows = near.shape[0] // count
    width = near.shape[1]
    step = min(rows, 64)
    each = width // sum(parts)
    taken = pl.BlockSpec((count, step, width), lambda i, p: (0, i, 0))
    wide = [2 * count * each * part for part in parts]
    return pl.pallas_call(
        functools.partial(spread_kernel, parts),
        grid_spec=pltpu.PrefetchScalarGridSpec(
            num_scalar_prefetch=1,
            grid=(rows // step,),
            in_specs=[taken, taken],
            out_specs=[pl.BlockSpec((step, w), lambda i, p: (i, 0)) for w in wide],
        ),
        out_shape=[jax.ShapeDtypeStruct((rows, w), F32) for w in wide],
        compiler_params=ROOM,
        cost_estimate=LIGHT,
        name="spread",
    )(places, near.reshape(count, rows, width), far.reshape(count, rows, width))


def place_kernel(places, blocks, *rest):
    rest[-1][...] = blocks[...].astype(F32)


def place_blocks(blocks, places, begun=None):
    count = lax.axis_size("head")
    rows, width = blocks.shape[0] // count, blocks.shape[1]
    extra = () if begun is None else (begun,)
    return pl.pallas_call(
        place_kernel,
        grid_spec=pltpu.PrefetchScalarGridSpec(
            num_scalar_prefetch=1,
            grid=(count,),
            in_specs=[pl.BlockSpec((rows, width), lambda r, p: (r, 0))]
            + [pl.BlockSpec(memory_space=pl.ANY) for _ in extra],
            out_specs=pl.BlockSpec((rows, width), lambda r, p: (0, p[r])),
        ),
        out_shape=jax.ShapeDtypeStruct((rows, 2 * count * width), F32),
        input_output_aliases={2: 0} if extra else {},
        compiler_params=ROOM,
        cost_estimate=LIGHT,
        name="place",
    )(places, blocks, *extra)


def turn(values, cosine, sine):
    low = values[:, : cosine.shape[1]]
    lane = lax.broadcasted_iota(jnp.int32, low.shape, 1)
    half = ROT // 2
    partner = jnp.where(
        lane < half, pltpu.roll(low, low.shape[1] - half, 1), pltpu.roll(low, half, 1)
    )
    return jnp.concatenate([low * cosine + partner * sine, values[:, cosine.shape[1] :]], axis=1)


def attention_kernel(
    order, first, qkv, bias, upstream, cosine, sine, context, context_rel, grads, keys, values,
    score, prob_grad, key_sum, value_sum,
):
    step = pl.program_id(0)
    total = pl.num_programs(0)
    size = HEAD_SIZE
    span = qkv.shape[1]
    last = (((1,), (1,)), ((), ()))
    rows = (((0,), (0,)), ((), ()))
    mine = order[step]
    start = first[step]
    cos_here, sin_here = cosine[mine], sine[mine]
    joined = qkv[0].astype(F32) + bias[...]
    query = (turn(joined[:, :size], cos_here, sin_here) * (size**-0.5)).astype(BF)
    at = pl.ds(pl.multiple_of(step * span, span), span)
    keys[at, :] = turn(joined[:, size : 2 * size], cos_here, sin_here).astype(BF)
    values[at, :] = joined[:, 2 * size :].astype(BF)
    key_sum[at, :] = jnp.zeros((span, size), F32)
    value_sum[at, :] = jnp.zeros((span, size), F32)
    up = upstream[0]

    def one(count):
        blocks = [slice(i * span, (i + 1) * span) for i in range(count)]
        top = jnp.full((span, 1), NEG_FILL, F32)
        for i, block in enumerate(blocks):
            part = lax.dot_general(query, keys[block, :], last, preferred_element_type=F32)
            if i == count - 1:
                row = lax.broadcasted_iota(jnp.int32, part.shape, 0)
                column = lax.broadcasted_iota(jnp.int32, part.shape, 1)
                part = jnp.where(column <= row, part, NEG_FILL)
            else:
                part = part + jnp.where(i >= start, 0.0, NEG_FILL)
            score[:, block] = part
            top = jnp.maximum(top, jnp.max(part, axis=1, keepdims=True))
        norm = jnp.zeros((span, 1), F32)
        for block in blocks:
            part = jnp.exp(score[:, block] - top)
            score[:, block] = part
            norm = norm + jnp.sum(part, axis=1, keepdims=True)
        inverse = 1.0 / norm
        out = jnp.zeros((span, size), F32)
        inner = jnp.zeros((span, 1), F32)
        for block in blocks:
            probs = score[:, block] * inverse
            score[:, block] = probs
            grad = lax.dot_general(up, values[block, :], last, preferred_element_type=F32)
            prob_grad[:, block] = grad
            inner = inner + jnp.sum(probs * grad, axis=1, keepdims=True)
            low = probs.astype(BF)
            out = out + jnp.dot(low, values[block, :], preferred_element_type=F32)
            value_sum[block, :] += lax.dot_general(low, up, rows, preferred_element_type=F32)
        context[0] = out.astype(BF)
        context_rel[0] = out.astype(BF)
        query_grad = jnp.zeros((span, size), F32)
        for block in blocks:
            low = (score[:, block] * (prob_grad[:, block] - inner)).astype(BF)
            query_grad = query_grad + jnp.dot(low, keys[block, :], preferred_element_type=F32)
            key_sum[block, :] += lax.dot_general(low, query, rows, preferred_element_type=F32)
        query_grad = (query_grad * (size**-0.5)).astype(BF).astype(F32)
        grads[mine, :, :size] = turn(query_grad, cos_here, -sin_here).astype(BF)

    steps = keys.shape[0] // span
    for index in range(steps):
        pl.when(step == index)(functools.partial(one, index + 1))

    @pl.when(step == total - 1)
    def finish():
        def each(index, carry):
            place = order[index]
            block = pl.ds(pl.multiple_of(index * span, span), span)
            key_grad = key_sum[block, :].astype(BF).astype(F32)
            grads[place, :, size : 2 * size] = turn(key_grad, cosine[place], -sine[place]).astype(
                BF
            )
            grads[place, :, 2 * size :] = value_sum[block, :].astype(BF)
            return carry

        lax.fori_loop(0, total, each, 0)


def attention(order, first, qkv, bias, upstream, cosine, sine):
    count, span, width = qkv.shape
    size = HEAD_SIZE
    length = count * span
    whole = lambda *shape: pl.BlockSpec(shape, lambda i, o, f: (0,) * len(shape))
    taken = lambda *shape: pl.BlockSpec(
        (1,) + shape, lambda i, o, f: (o[i],) + (0,) * len(shape)
    )
    pairs = count * (count + 1) // 2
    return pl.pallas_call(
        attention_kernel,
        grid_spec=pltpu.PrefetchScalarGridSpec(
            num_scalar_prefetch=2,
            grid=(count,),
            in_specs=[
                taken(span, width),
                whole(1, width),
                taken(span, size),
                whole(count, span, cosine.shape[-1]),
                whole(count, span, cosine.shape[-1]),
            ],
            out_specs=[
                pl.BlockSpec((1, span, size), lambda i, o, f: (i, 0, 0)),
                taken(span, size),
                whole(count, span, width),
            ],
            scratch_shapes=[
                pltpu.VMEM((length, size), BF),
                pltpu.VMEM((length, size), BF),
                pltpu.VMEM((span, length), F32),
                pltpu.VMEM((span, length), F32),
                pltpu.VMEM((length, size), F32),
                pltpu.VMEM((length, size), F32),
            ],
        ),
        out_shape=[
            jax.ShapeDtypeStruct((count, span, size), BF),
            jax.ShapeDtypeStruct((count, span, size), BF),
            jax.ShapeDtypeStruct((count, span, width), BF),
        ],
        compiler_params=ROOM,
        cost_estimate=LIGHT,
        name="attention",
    )(order, first, qkv, bias, upstream, cosine, sine)


def segment_start(lengths, at):
    lengths = lengths.reshape(-1)
    starts = jnp.stack([jnp.sum(lengths[:i]) for i in range(lengths.shape[0])])
    return jnp.max(jnp.where(starts[None, :] <= at[:, None], starts[None, :], 0), axis=1).astype(
        jnp.int32
    )


def rotary_tables(lengths, places, span):
    at = places * span
    offset = (at - segment_start(lengths, at))[:, None] + jnp.arange(span, dtype=jnp.int32)[None, :]
    half = ROT // 2
    frequency = ROT_BASE ** (-(2.0 * jnp.arange(half, dtype=F32)) / ROT)
    angles = offset.astype(F32)[..., None] * frequency
    cosine, sine = jnp.cos(angles), jnp.sin(angles)
    rest = jnp.zeros(offset.shape + (128 - ROT,), F32)
    return (
        jnp.concatenate([cosine, cosine, rest + 1.0], axis=-1),
        jnp.concatenate([-sine, sine, rest], axis=-1),
    )


def body(
    block_in,
    cotangent,
    seg_lengths,
    ln1_gain,
    ln1_bias,
    qkv_weight,
    qkv_bias,
    out_weight,
    out_bias,
    ln2_gain,
    ln2_bias,
    fc1_weight,
    fc1_bias,
    fc2_weight,
    fc2_bias,
):
    rows_here, span, width = block_in.shape
    shard, hidden_units = fc1_weight.shape
    data_count = lax.axis_size("dp")
    head_count = lax.axis_size("head")
    blk_count = lax.axis_size("blk")
    plane = head_count * blk_count
    head_place = lax.axis_index("head")
    blk_place = lax.axis_index("blk")
    place = head_place * blk_count + blk_place
    each = hidden_units // plane
    length = plane * span

    places = [
        (head_place ^ (r % head_count)) * blk_count + (blk_place ^ (r // head_count))
        for r in range(plane)
    ]
    place_list = jnp.stack(places).astype(jnp.int32)
    absolute = jnp.arange(plane, dtype=jnp.int32)
    order = (absolute % blk_count ^ blk_place) * head_count + (absolute // blk_count ^ head_place)

    def columns(values, wide):
        return lax.dynamic_slice_in_dim(values, place * wide, wide, 1)

    own_in = block_in.reshape(span, width)
    own_up = cotangent.reshape(span, width)
    att_shard = jnp.concatenate(
        [
            columns(qkv_weight[:, part * width : (part + 1) * width], HEAD_SIZE)
            for part in range(3)
        ]
        + [columns(out_weight, HEAD_SIZE)],
        axis=1,
    )
    att_shard, own_in = tie(att_shard, own_in)
    att_mine = data_gather(att_shard)
    tokens_begun = gather_start(own_in)
    tokens_begun, own_up = tie(tokens_begun, own_up)
    upstream_begun = gather_start(own_up)
    tokens_near, tokens_far = gather_end(*gather_middle(*tokens_begun))
    fc1_shard, tokens_near = tie(columns(fc1_weight, each), tokens_near)
    fc1_mine = data_gather(fc1_shard)
    cosine, sine = rotary_tables(seg_lengths, jnp.stack(places), span)
    normed, attn_in, mlp_in = norms(
        tokens_near, tokens_far, span, ln1_gain, ln1_bias, ln2_gain, ln2_bias
    )
    upstream_begun, attn_in, cosine, sine = tie(upstream_begun, attn_in, cosine, sine)
    upstream_near, upstream_far = gather_end(*gather_middle(*upstream_begun))
    upstream_near, att_mine, attn_in = tie(upstream_near, att_mine, attn_in)
    qkv_mine, out_mine = att_mine[:, : 3 * HEAD_SIZE], att_mine[:, 3 * HEAD_SIZE :]
    out_rows = lax.all_to_all(out_mine, ("head", "blk"), split_axis=0, concat_axis=1, tiled=True)

    first = segment_start(seg_lengths, absolute * span) // span

    joined = product(attn_in, qkv_mine, NN, kind=F32)
    upstream_near, upstream_far, joined, out_rows = tie(
        upstream_near, upstream_far, joined, out_rows
    )
    upstream = jnp.concatenate([upstream_near, upstream_far], axis=0)
    context_grad = product(upstream, out_rows, NT)
    bias_mine = jnp.concatenate(
        [
            lax.dynamic_slice_in_dim(qkv_bias, part * width + place * HEAD_SIZE, HEAD_SIZE, 0)
            for part in range(3)
        ]
    ).astype(F32)
    context_abs, context, qkv_grad = attention(
        order.astype(jnp.int32),
        first,
        joined.reshape(plane, span, 3 * HEAD_SIZE),
        bias_mine[None, :],
        context_grad.reshape(plane, span, HEAD_SIZE),
        cosine,
        sine,
    )
    context = context.reshape(length, HEAD_SIZE)
    qkv_grad = qkv_grad.reshape(length, 3 * HEAD_SIZE)
    out_grad = wide_product(context, upstream)
    out_grad = lax.all_to_all(out_grad, ("head", "blk"), split_axis=1, concat_axis=0, tiled=True)
    qkv_w_grad = product(attn_in, qkv_grad, TN)
    att_grad = jnp.concatenate([qkv_w_grad, out_grad], axis=1)

    fc1_mine, att_grad, context_abs, out_mine, fc2_shard = tie(
        fc1_mine, att_grad, context_abs, out_mine, columns(fc2_weight, each)
    )
    chain = data_count == 4
    if chain:
        move_one = exchange_one(fc2_shard, att_grad)
    else:
        fc2_mine, att_sum = data_gather(fc2_shard), data_scatter(att_grad)
    out_moved = gather_start(out_mine)
    fc1_bias_mine = lax.dynamic_slice_in_dim(fc1_bias, place * each, each, 0).astype(F32)
    active, slope = hidden_units_of(mlp_in, fc1_mine, fc1_bias_mine[None, :])
    if chain:
        move_one, out_moved, fc2_shard, att_grad, active = tie(
            move_one, out_moved, fc2_shard, att_grad, active
        )
        move_two = exchange_two(fc2_shard, att_grad, *move_one)
    out_moved = gather_middle(*out_moved)
    fc2_grad = product(upstream, active, TN)
    if chain:
        move_two, out_moved, att_grad, fc2_grad, context_abs = tie(
            move_two, out_moved, att_grad, fc2_grad, context_abs
        )
        move_three = exchange_three(att_grad, *move_two)
    own_context = lax.all_to_all(
        context_abs.reshape(length, HEAD_SIZE),
        ("head", "blk"),
        split_axis=0,
        concat_axis=1,
        tiled=True,
    )
    if chain:
        move_three, att_grad, own_context, out_moved = tie(
            move_three, att_grad, own_context, out_moved
        )
        move_four = exchange_four(att_grad, *move_three)
    if chain:
        move_four, fc2_grad = tie(move_four, fc2_grad)
        att_sum, fc2_mine = exchange_end(
            fc2_shard, att_grad, move_one, move_two, move_three, move_four
        )
    fc2_sum = data_scatter(fc2_grad)

    att_moved = gather_start(att_sum)
    mlp_far = product_far(active, fc2_mine)
    mlp_got = other_core(mlp_far)
    hidden_grad, fc1_bias_part = hidden_grad_of(upstream, fc2_mine, slope)
    att_moved, mlp_got, hidden_grad, active = tie(att_moved, mlp_got, hidden_grad, active)
    att_moved = gather_middle(*att_moved)
    mlp_parts = product_near(active, fc2_mine, mlp_got, span)
    att_moved, mlp_parts, hidden_grad = tie(att_moved, mlp_parts, hidden_grad)
    mlp_got = collect_start(*mlp_parts)
    fc1_grad = product(mlp_in, hidden_grad, TN)
    att_near, out_near = join(*att_moved), join(*out_moved)
    mlp_got, fc1_grad, hidden_grad, fc2_sum, att_near, out_near = tie(
        mlp_got, fc1_grad, hidden_grad, fc2_sum, att_near, out_near
    )
    fc1_sum = data_scatter(fc1_grad)
    mlp_done = collect_middle(mlp_parts, mlp_got)
    att_far, out_far = other_core(att_near), other_core(out_near)
    gains = (ln1_gain.astype(F32)[None, :], ln2_gain.astype(F32)[None, :])
    share_far, sums_far = shares(
        False, qkv_grad, qkv_mine, hidden_grad, fc1_mine, gains, normed, span
    )
    mlp_done, share_far, att_far, out_far, fc2_sum = tie(
        mlp_done, share_far, att_far, out_far, fc2_sum
    )
    share_got = other_core(share_far)
    fc2_moved = gather_start(fc2_sum)
    *share_parts, sums_near = shares(
        True, qkv_grad, qkv_mine, hidden_grad, fc1_mine, gains, normed, span, share_got
    )
    fc2_moved, share_parts, att_far, out_far = tie(fc2_moved, share_parts, att_far, out_far)
    share_got = collect_start(*share_parts)
    fc2_moved = gather_middle(*fc2_moved)
    attn_out = columns_product(own_context, out_near, out_far, place_list) + out_bias
    qkv_out, out_out = spread_columns(att_near, att_far, place_list, (3, 1))
    mlp_out = collect_end(*mlp_done) + fc2_bias
    own_float = own_in.astype(F32)
    block_out = (own_float + attn_out + mlp_out).astype(BF).reshape(block_in.shape)

    moves = sum_moves()
    qkv_bias_part = jnp.sum(qkv_grad.astype(F32), axis=0).reshape(3, 1, HEAD_SIZE)
    here = (jnp.arange(plane) == place).astype(F32)
    norm_sums = sums_far + sums_near
    terms = (
        norm_sums[0],
        norm_sums[1],
        (qkv_bias_part * here[None, :, None]).reshape(-1),
        jnp.sum(own_up.astype(F32), axis=0),
        norm_sums[2],
        norm_sums[3],
        (here[:, None] * fc1_bias_part).reshape(-1),
        jnp.stack([jnp.sum(attn_out * attn_out), jnp.sum(mlp_out * mlp_out)]),
    )
    sizes = [term.shape[0] for term in terms]
    vector = jnp.concatenate(terms + (jnp.zeros((-sum(sizes) % 1024,), F32),)).reshape(-1, 128)
    share_got, fc2_moved, vector, block_out, qkv_out, out_out, fc1_sum = tie(
        share_got, fc2_moved, vector, block_out, qkv_out, out_out, fc1_sum
    )
    share_done = collect_middle(share_parts, share_got)
    fc1_moved = gather_start(fc1_sum)
    vector = sum_move(sum_move(vector, moves[0]), moves[1])
    fc2_near = join(*fc2_moved)
    share_done, fc1_moved, vector, fc2_near = tie(share_done, fc1_moved, vector, fc2_near)
    fc1_moved = gather_middle(*fc1_moved)
    fc2_far = other_core(fc2_near)
    fc2_out = place_blocks(fc2_near, place_list[:head_count])
    vector = sum_move(vector, moves[2])

    share = collect_end(*share_done)
    own_centred = own_float - jnp.mean(own_float, axis=-1, keepdims=True)
    own_scaled = lax.rsqrt(jnp.mean(own_centred * own_centred, axis=-1, keepdims=True) + NORM_EPS)
    own_normed = own_centred * own_scaled
    share = own_scaled * (
        share
        - jnp.mean(share, axis=-1, keepdims=True)
        - own_normed * jnp.mean(share * own_normed, axis=-1, keepdims=True)
    )
    input_grad = (own_up.astype(F32) + share).astype(BF).reshape(block_in.shape)

    fc1_moved, vector, fc2_out, fc2_far, input_grad = tie(
        fc1_moved, vector, fc2_out, fc2_far, input_grad
    )
    fc1_near, fc1_far = gather_end(*fc1_moved)
    fc2_out = place_blocks(fc2_far, place_list[head_count:], fc2_out)
    fc1_out = place_blocks(fc1_near, place_list[:head_count])
    for move in moves[3:]:
        vector = sum_move(vector, move)
    fc1_far, fc1_out, fc2_out, vector = tie(fc1_far, fc1_out, fc2_out, vector)
    fc1_out = place_blocks(fc1_far, place_list[head_count:], fc1_out)
    reduced = [
        vector.reshape(-1)[sum(sizes[:i]) : sum(sizes[: i + 1])] for i in range(len(sizes))
    ]
    entries = rows_here * length * data_count * width
    branch_rms = jnp.sqrt(reduced[7] / entries)
    return (
        block_out,
        input_grad,
        reduced[0],
        reduced[1],
        qkv_out,
        reduced[2],
        out_out,
        reduced[3],
        reduced[4],
        reduced[5],
        fc1_out,
        reduced[6],
        fc2_out,
        reduced[3],
        branch_rms[0],
        branch_rms[1],
    )


def solution(mesh):
    rows, tokens, whole = P("dp", None), P("dp", ("head", "blk"), None), P()
    return jax.shard_map(
        body,
        mesh=mesh,
        in_specs=(
            tokens,
            tokens,
            rows,
            whole,
            whole,
            rows,
            whole,
            rows,
            whole,
            whole,
            whole,
            rows,
            whole,
            rows,
            whole,
        ),
        out_specs=(
            tokens,
            tokens,
            whole,
            whole,
            rows,
            whole,
            rows,
            whole,
            whole,
            whole,
            rows,
            whole,
            rows,
            whole,
            whole,
            whole,
        ),
        check_vma=False,
    )
```
